128 devices in a mesh: row: 8 (over z, core), col: 16 (over y, x).
Axes of the slice: x: 4, y: 4, z: 4, core: 2. Of those that a mesh axis runs over, the one named last changes fastest.
Arguments:
- covariance: float32 [4, 8, 2, 16, 512, 512], P(None, 'row', None, 'col'), may hold values from 0 to 9.5, as said below
- migration: int32 [8, 16, 16], replicated, may hold values from -1 to 15, as said below
Outputs:
- factor: float32 [4, 8, 2, 16, 512, 512], P(None, 'row', None, 'col')
- offloaded: float32 [8, 16, 16, 512, 256], P('row', 'col')
The draws below stay inside these ranges and needn't reach their ends.
Inputs may be any that keep to these rules, and one draw needn't show every extreme that they name: covariance is symmetric and positive definite, with smallest eigenvalue 0.5 or more. An entry t >= 0 of migration[r, s, d] names half t % 2 of the local tile t // 2 of device (r, s), and that tile A[i, j] has i >= j > 1; each half-tile is named at most once; migration[r, s, s] = -1.
All inputs are finite; a program needn't handle non-finite values.
Results may differ from the reference program's by a relative error of at most 0.0003.
Values sent between devices are 32-bit elements; how exact they have to be, the bound alone decides.
A program may use at most 192 MiB of HBM per device.

```python
import jax
import jax.numpy as jnp
from jax import lax

NB = 512
HALF = 256
TR = 4
TC = 2
TILES = 32
ORDER = 16384
N_ROW = 8
N_COL = 16


nugget = 0.5


def draw_covariance(key, part):
    key = jax.random.fold_in(key, 11)
    points = jax.random.uniform(key, (ORDER, 3), jnp.float32)
    length = 0.25
    squared = jnp.zeros((ORDER, ORDER), jnp.float32)
    for coord in range(3):
        diff = points[:, None, coord] - points[None, :, coord]
        squared = squared + diff * diff
    kernel = jnp.exp(-jnp.sqrt(squared) / length)
    kernel = kernel + nugget * jnp.eye(ORDER, dtype=jnp.float32)
    rows_grid = TILES // TR
    cols_grid = TILES // TC
    shaped = kernel.reshape(TR, rows_grid, NB, TC, cols_grid, NB)
    return shaped.transpose(0, 1, 3, 4, 2, 5)


def draw_migration(key, part):
    key = jax.random.fold_in(key, 29)
    rows_grid = TILES // TR
    cols_grid = TILES // TC
    halves = 2 * TR * TC
    slot = jnp.arange(halves, dtype=jnp.int32)
    tile_id = slot // 2
    grid_r = jnp.arange(rows_grid, dtype=jnp.int32)[:, None, None]
    grid_c = jnp.arange(cols_grid, dtype=jnp.int32)[None, :, None]
    i_tile = (tile_id // TC)[None, None, :] * rows_grid + grid_r
    j_tile = (tile_id % TC)[None, None, :] * cols_grid + grid_c
    active = ((i_tile >= j_tile) & (j_tile > 1)).astype(jnp.int32)
    noise = jax.random.randint(jax.random.fold_in(key, 1), (rows_grid, cols_grid, halves), 0, halves, jnp.int32)
    not_last = (slot != halves - 1).astype(jnp.int32)[None, None, :]
    score = (1 - active) * (4 * halves * halves) + not_last * (noise * halves + slot[None, None, :] + halves)
    order = jnp.argsort(score, axis=-1, stable=True).astype(jnp.int32)
    number = jnp.minimum(jnp.sum(active, axis=-1) // 2, cols_grid - 1)
    target = jnp.arange(cols_grid, dtype=jnp.int32)[None, None, :]
    own = (target == grid_c).astype(jnp.int32)
    noise_two = jax.random.randint(jax.random.fold_in(key, 2), (rows_grid, cols_grid, cols_grid), 0, cols_grid, jnp.int32)
    score_two = own * (2 * cols_grid * cols_grid) + noise_two * cols_grid + target
    target_order = jnp.argsort(score_two, axis=-1, stable=True).astype(jnp.int32)
    rank = jnp.argsort(target_order, axis=-1, stable=True).astype(jnp.int32)
    chosen = jnp.take_along_axis(order, jnp.minimum(rank, halves - 1), axis=-1)
    return jnp.where(rank < number[:, :, None], chosen, -1).astype(jnp.int32)


def setup_inputs(seed: int = 0) -> dict:
    splits = jax.random.split(jax.random.key(seed), 3)
    return {
        "covariance": draw_covariance(jax.random.fold_in(splits[2], 71), 0),
        "migration": draw_migration(jax.random.fold_in(splits[2], 71), 0),
    }


def solve_panel(lower, panel):
    count = panel.shape[0]
    block = panel.shape[1]
    wide = panel.transpose(2, 0, 1).reshape(block, count * block)
    solved = lax.linalg.triangular_solve(lower, wide, left_side=True, lower=True)
    return solved.reshape(block, count, block).transpose(1, 2, 0)

def reference(covariance, migration):
    tiles = covariance.reshape(TILES, TILES, NB, NB)
    index = jnp.arange(TILES, dtype=jnp.int32)
    panel = None
    for step in range(2):
        lower = jnp.linalg.cholesky(tiles[step, step])
        solved = solve_panel(lower, tiles[:, step])
        panel = jnp.where((index > step)[:, None, None], solved, jnp.where((index == step)[:, None, None], lower[None], jnp.zeros_like(solved)))

        def row_update(operands):
            tile_row, left, place = operands
            product = jnp.einsum('ab,jcb->jac', left, panel, precision=lax.Precision.HIGHEST)
            active = (place >= index) & (index > step)
            return jnp.where(active[:, None, None], tile_row - product, tile_row)
        tiles = lax.map(row_update, (tiles, panel, index))
        column = jnp.where((index >= step)[:, None, None], panel, tiles[:, step])
        tiles = tiles.at[:, step].set(column)
    upper = index[:, None] < index[None, :]
    tiles = jnp.where(upper[:, :, None, None], jnp.zeros_like(tiles), tiles)
    flat_plan = migration.transpose(0, 2, 1).reshape(N_ROW * N_COL, N_COL)
    place_rows = (jnp.arange(N_ROW * N_COL, dtype=jnp.int32) // N_COL).astype(jnp.int32)
    sources = jnp.arange(N_COL, dtype=jnp.int32)

    def one_place(operands):
        entries, place_r = operands
        chosen = jnp.maximum(entries, 0)
        tile_id = chosen // 2
        i_tile = tile_id // TC * N_ROW + place_r
        j_tile = tile_id % TC * N_COL + sources
        left = jnp.take(panel, i_tile, axis=0)
        right = jnp.take(panel, j_tile, axis=0)
        right_half = jnp.where((chosen % 2 == 0)[:, None, None], right[:, :HALF], right[:, HALF:])
        product = jnp.einsum('sae,sbe->sab', left, right_half, precision=lax.Precision.HIGHEST)
        return jnp.where((entries >= 0)[:, None, None], product, jnp.zeros_like(product))
    offloaded = lax.map(one_place, (flat_plan, place_rows)).reshape(N_ROW, N_COL, N_COL, NB, HALF)
    return (tiles.reshape(covariance.shape), offloaded)
```

```python
import functools

import jax
import jax.numpy as jnp
from jax import lax
from jax.experimental import pallas as pl
from jax.experimental.pallas import tpu as pltpu
from jax.sharding import PartitionSpec as P

NB = 512
QB = 128
HALF = 256
MESH = pl.DeviceIdType.MESH
EXACT = lax.Precision.HIGHEST
F32 = jnp.float32
BF16 = jnp.bfloat16
ANY = pl.BlockSpec(memory_space=pl.ANY)
VMEM = pl.BlockSpec(memory_space=pltpu.VMEM)
SMEM = pl.BlockSpec(memory_space=pltpu.SMEM)

PARTS3 = ((0, 176, 88, "xyz"), (176, 168, 88, "yzx"), (344, 168, 88, "zxy"))
PARTS2 = ((0, 256, 128, "xy"), (256, 256, 128, "yx"))
TREE_TILE = ((0, 176, "xyz"), (176, 168, "yzx"), (344, 168, "zxy"))
TREE_PANEL = ((0, 48, "xyz"), (48, 40, "yzx"), (88, 40, "zxy"))
AHEAD = 2


def dot(a, b):
    return lax.dot_general(
        a, b, (((1,), (0,)), ((), ())), precision=EXACT, preferred_element_type=F32
    )


def dot_nt(a, b):
    return lax.dot_general(
        a, b, (((1,), (1,)), ((), ())), precision=EXACT, preferred_element_type=F32
    )


def lane_spread(v, j):
    return jnp.broadcast_to(v[:, j : j + 1], (8, 128))


def row_spread(v, i):
    return jnp.broadcast_to(v[i : i + 1, :], (8, 128))


def factor128(rows):
    n = len(rows)
    lane = lax.broadcasted_iota(jnp.int32, (8, 128), 1)
    sub = lax.broadcasted_iota(jnp.int32, (8, 128), 0)
    s_rows = list(rows)
    e_rows = [jnp.where(lane == sub + 8 * i, 1.0, 0.0).astype(F32) for i in range(n)]
    upper, inverse = [], []
    zero = jnp.zeros((8, 256), F32)
    for k in range(n):
        cols = [lane_spread(s_rows[k], 8 * k + j) for j in range(8)]
        a = [[row_spread(cols[j], i) if i >= j else None for j in range(8)] for i in range(8)]
        s = [row_spread(s_rows[k], j) for j in range(8)]
        e = [row_spread(e_rows[k], j) for j in range(8)]
        r = [None] * 8
        m = [[None] * 8 for _ in range(8)]
        for j in range(0, 8, 2):
            p, b, c = a[j][j], a[j + 1][j], a[j + 1][j + 1]
            r[j] = 1.0 / p
            r[j + 1] = p * (1.0 / (p * c - b * b))
            for i in range(j + 1, 8):
                m[i][j] = a[i][j] * r[j]
            for i in range(j + 1, 8):
                a[i][j + 1] = a[i][j + 1] - m[i][j] * b
            for i in range(j + 2, 8):
                m[i][j + 1] = a[i][j + 1] * r[j + 1]
            for i in range(j + 2, 8):
                for q in range(j + 2, i + 1):
                    a[i][q] = a[i][q] - m[i][j] * a[q][j] - m[i][j + 1] * a[q][j + 1]
        for j in range(8):
            for i in range(j + 1, 8):
                s[i] = s[i] - m[i][j] * s[j]
                e[i] = e[i] - m[i][j] * e[j]
        u = jnp.zeros((8, 128), F32)
        x = u
        for j in range(8):
            scale = lax.rsqrt(a[j][j])
            u = jnp.where(sub == j, s[j] * scale, u)
            x = jnp.where(sub == j, e[j] * scale, x)
        upper.append(jnp.where(lane >= sub + 8 * k, u, 0.0))
        inverse.append(x)
        if k + 1 == n:
            continue
        ws, we = [None] * 8, [None] * 8
        for j in range(7, -1, -1):
            ws[j] = s[j] * r[j]
            we[j] = e[j] * r[j]
            for i in range(j + 1, 8):
                ws[j] = ws[j] - m[i][j] * ws[i]
                we[j] = we[j] - m[i][j] * we[i]
        last = min(n, k + 1 + AHEAD)
        if last < n:
            w, v = u * 0.0, u * 0.0
            for j in range(8):
                w = jnp.where(sub == j, ws[j], w)
                v = jnp.where(sub == j, we[j], v)
            wide = [zero] * k + [jnp.concatenate([w, v], 1)] + [zero] * (n - 1 - k)
            change = dot(jnp.concatenate(s_rows[last:], 0), jnp.concatenate(wide, 0))
        for i in range(k + 1, last):
            c = [lane_spread(s_rows[i], 8 * k + j) for j in range(8)]
            t, v = s_rows[i], e_rows[i]
            for j in range(8):
                t = t - c[j] * ws[j]
                v = v - c[j] * we[j]
            s_rows[i], e_rows[i] = t, v
        for i in range(last, n):
            g = change[8 * (i - last) : 8 * (i - last) + 8]
            s_rows[i] = s_rows[i] - g[:, :128]
            e_rows[i] = e_rows[i] - g[:, 128:]
    return jnp.concatenate(upper, 0), jnp.concatenate(inverse, 0)


def unit(ref):
    row = lax.broadcasted_iota(jnp.int32, (NB, NB), 0)
    col = lax.broadcasted_iota(jnp.int32, (NB, NB), 1)
    ref[...] = jnp.where(row == col, 1.0, 0.0).astype(F32)


def factor_panel(p, s_ref, x_ref, u_ref):
    base = pl.multiple_of(p * 128, 128)
    here = pl.ds(base, 128)
    rows = [s_ref[pl.ds(pl.multiple_of(base + 8 * i, 8), 8), here] for i in range(16)]
    upper, inverse = factor128(rows)
    across = dot(inverse, s_ref[here, :])
    place = lax.broadcasted_iota(jnp.int32, (128, NB), 1)
    u_ref[here, :] = jnp.where(place >= base + 128, across, 0.0)
    u_ref[here, here] = upper
    xrow = dot(inverse, x_ref[here, :])
    x_ref[here, :] = xrow

    @pl.when(p < 3)
    def _():
        below = dot_nt(s_ref[:, here], inverse)
        place = lax.broadcasted_iota(jnp.int32, (NB, 128), 0)
        below = jnp.where(place >= base + 128, below, 0.0)
        s_ref[...] = s_ref[...] - dot(below, across)
        x_ref[...] = x_ref[...] - dot(below, xrow)


def exchange_kernel(
    cov_ref, g_ref, r0_ref, c0_ref, x00_out, x11_out, u00_out, u11_out,
    s_ref, x_ref, u_ref, x11_ref, u11_ref, a10_ref, a11_ref, own_ref, blk_ref, tile_ref,
    local_sem, sc_send, sc_recv, tx_send, tx_recv, ta_send, ta_recv,
    row_send, row_recv, ag_send, ag_recv, sib_send, sib_recv, c_send, c_recv, near_send, near_recv,
):
    row = lax.axis_index("row")
    col = lax.axis_index("col")
    z, core = row // 2, row % 2
    y, x = col // 4, col % 4
    pos = {"x": x, "y": y, "z": z}

    def along(axis, delta):
        q = dict(pos)
        q[axis] = (q[axis] + delta) % 4
        return (q["z"] * 2 + core, q["y"] * 4 + q["x"])

    sibling = (z * 2 + (1 - core), col)

    def remote(src, dst, target, ssem, rsem):
        return pltpu.make_async_remote_copy(
            src_ref=src, dst_ref=dst, send_sem=ssem, recv_sem=rsem, device_id=target, device_id_type=MESH
        )

    def local(src, dst):
        c = pltpu.make_async_copy(src, dst, local_sem)
        c.start()
        c.wait()

    is_root = (row == 0) & (col == 0)
    source_col = (y % 2) * 8 + row
    is_source = row < 2
    self0 = is_root
    self1 = (row == 1) & (col == 1)
    selfish = self0 | self1

    def scatter_target(m, q):
        l = 2 * m + col // 8
        return (col % 8, l * 4 + q), l

    barrier = pltpu.get_barrier_semaphore()

    def greet(target):
        pl.semaphore_signal(barrier, inc=1, device_id=target, device_id_type=MESH)

    for axis in "xyz":
        for delta in (1, 2, 3):
            greet(along(axis, delta))
    greet(sibling)
    pl.when(jnp.logical_not(self0))(lambda: greet((0, source_col)))
    pl.when(jnp.logical_not(self1))(lambda: greet((1, source_col)))

    def is_self(m, q):
        target, _ = scatter_target(m, q)
        return (target[0] == row) & (target[1] == col)

    @pl.when(is_source)
    def _():
        for m in range(2):
            for q in range(4):
                target, _ = scatter_target(m, q)
                pl.when(jnp.logical_not(is_self(m, q)))(functools.partial(greet, target))

    is_source_i = is_source.astype(jnp.int32)
    selfish_i = selfish.astype(jnp.int32)
    pl.semaphore_wait(barrier, 12 + 8 * is_source_i - 2 * selfish_i)

    def scatter_copy(m, q, dst, rsem):
        target, _ = scatter_target(m, q)
        return remote(cov_ref.at[0, m, :, pl.ds(128 * q, 128)], dst, target, sc_send.at[m * 4 + q], rsem)

    for which in range(2):

        @pl.when(row == which)
        def _(which=which):
            for m in range(2):
                for q in range(4):
                    _, l = scatter_target(m, q)
                    if which == 0:
                        copy = scatter_copy(m, q, r0_ref.at[l, q], sc_recv.at[0])
                    else:
                        copy = scatter_copy(m, q, own_ref, sc_recv.at[1])
                    pl.when(jnp.logical_not(is_self(m, q)))(copy.start)

    def offsets(root):
        return {a: (pos[a] - root[a] + 4) % 4 for a in "xyz"}

    def level(order, d):
        return jnp.where(
            d[order[2]] != 0, 2, jnp.where(d[order[1]] != 0, 1, jnp.where(d[order[0]] != 0, 0, -1))
        )

    def tree(parts, root, piece, ssem, rsem):
        d = offsets(root)
        levels = [level(order, d) for (_, _, order) in parts]

        def copy(i, t, k):
            r0, n, order = parts[i]
            return remote(piece(r0, n), piece(r0, n), along(order[t], k + 1), ssem(i, t * 3 + k), rsem(i))

        def arrive(s):
            for i in range(3):

                @pl.when(levels[i] == s)
                def _(i=i):
                    copy(i, 0, 0).wait_recv()
                    for t in range(s + 1, 3):
                        for k in range(3):
                            copy(i, t, k).start()

        def begin():
            for t in range(3):
                for i in range(3):
                    for k in range(3):
                        copy(i, t, k).start()

        def sent():
            for i in range(3):
                for t in range(3):

                    @pl.when(levels[i] < t)
                    def _(i=i, t=t):
                        for k in range(3):
                            copy(i, t, k).wait_send()

        return begin, arrive, sent

    zero_root = {"x": 0, "y": 0, "z": 0}
    tile_trees = []
    for i, (ref, at) in enumerate(((a10_ref, {"x": 0, "y": 0, "z": 0}), (a11_ref, {"x": 1, "y": 0, "z": 0}))):
        tile_trees.append(
            tree(
                TREE_TILE, at,
                lambda r0, n, ref=ref: ref.at[pl.ds(r0, n), :],
                lambda j, k, i=i: ta_send.at[i, j, k],
                lambda j, i=i: ta_recv.at[i, j],
            )
        )
    def tiles_arrive(level):
        @pl.when(core == 1)
        def _():
            for t in tile_trees:
                t[1](level)

    for i, ref in enumerate((a10_ref, a11_ref)):

        @pl.when((row == 1) & (col == i))
        def _(i=i, ref=ref):
            local(cov_ref.at[0, 0], ref)
            tile_trees[i][0]()

    @pl.when(is_root)
    def _():
        local(cov_ref.at[0, 0], s_ref)
        local(s_ref.at[:, pl.ds(0, 128)], r0_ref.at[0, 0])
        unit(x11_ref)

    @pl.when(jnp.logical_not(is_root))
    def _():
        u_ref[...] = jnp.zeros((NB, NB), F32)

    @pl.when(self1)
    def _():
        local(cov_ref.at[0, 0, :, pl.ds(128, 128)], own_ref)

    @pl.when(jnp.logical_not(self0))
    def _():
        remote(r0_ref.at[y, x], r0_ref.at[y, x], (0, source_col), sc_send.at[0], sc_recv.at[0]).wait_recv()

    def gather(parts, view, own, ssem, rsem, sib=None):
        phases = len(parts[0][3])

        def part_view(order, k, delta, r0, n, c=core):
            at = {}
            for j, a in enumerate(order):
                if j < k:
                    at[a] = slice(None)
                elif j == k:
                    at[a] = (pos[a] + delta) % 4
                else:
                    at[a] = pos[a]
            return view(at, r0, n, c)

        def number(k, i):
            return (k * len(parts) + i) * 4

        def direct(k, i, j):
            r0, n, h, order = parts[i]
            m = number(k, i)
            dst = part_view(order, k, 0, r0, n)
            src = own(r0, n) if k == 0 else dst
            return remote(src, dst, along(order[k], (1, 3)[j]), ssem.at[m + j], rsem.at[m + j])

        def passed(k, i, j, back):
            r0, n, h, order = parts[i]
            m = number(k, i) + 2 + j
            q0, qn = ((r0, h), (r0 + h, n - h))[j]
            half = part_view(order, k, back, q0, qn)
            return remote(half, half, along(order[k], (1, 3)[j]), ssem.at[m], rsem.at[m])

        def send(k):
            for i in range(len(parts)):
                for j in range(2):
                    direct(k, i, j).start()

        def forward(k):
            for i, (r0, n, h, order) in enumerate(parts):
                m = number(k, i)
                for j, back in ((0, 3), (1, 1)):
                    got = part_view(order, k, back, r0, n)
                    remote(got, got, along(order[k], 1), ssem.at[m + j], rsem.at[m + j]).wait_recv()
                    passed(k, i, j, back).start()
                    if sib:
                        sib(got, 3 + k * 9 + i * 2 + j).start()

        def finish(k):
            for i, (r0, n, h, order) in enumerate(parts):
                for j in range(2):
                    passed(k, i, j, 2).wait_recv()
                if sib:
                    sib(part_view(order, k, 2, r0, n), 3 + k * 9 + 6 + i).start()

        def sent():
            for k in range(phases):
                for i in range(len(parts)):
                    for j in range(2):
                        direct(k, i, j).wait_send()
                        passed(k, i, j, 2).wait_send()

        def pair_views(c):
            views = [part_view(order, 0, 0, r0, n, c) for (r0, n, h, order) in parts]
            for k in range(phases):
                for r0, n, h, order in parts:
                    views.append(part_view(order, k, 3, r0, n, c))
                    views.append(part_view(order, k, 1, r0, n, c))
                for r0, n, h, order in parts:
                    views.append(part_view(order, k, 2, r0, n, c))
            return views

        return send, forward, finish, sent, pair_views

    row_send_step, row_forward, row_finish, row_sent, _ = gather(
        PARTS2,
        lambda at, r0, n, c: r0_ref.at[at["y"], at["x"], pl.ds(r0, n), :],
        lambda r0, n: r0_ref.at[y, x, pl.ds(r0, n), :],
        row_send, row_recv,
    )

    row_send_step(0)

    def chol_one(p, carry):
        @pl.when(is_root)
        def _():
            factor_panel(p, s_ref, x11_ref, u_ref)
            x_ref[panel_rows(p), :] = x11_ref[panel_rows(p), :]
            begin, _, sent = panel_tree(p)

            @pl.when(p > 0)
            def _():
                sent()
                to_sibling(p).wait_send()

            begin()
            to_sibling(p).start()

        @pl.when(p == 0)
        def _():
            tiles_arrive(0)
            row_forward(0)

        @pl.when(p == 1)
        def _():
            tiles_arrive(1)
            row_finish(0)
            row_send_step(1)

        @pl.when(p == 2)
        def _():
            tiles_arrive(2)

            @pl.when(core == 1)
            def _():
                for i, ref in enumerate((a10_ref, a11_ref)):
                    remote(ref, ref, sibling, near_send.at[4 + i], near_recv.at[4 + i]).start()

            row_forward(1)

        return carry

    def panel_rows(p):
        return pl.ds(pl.multiple_of(p * 128, 128), 128)

    def panel_tree(p):
        return tree(
            TREE_PANEL, zero_root,
            lambda r0, n: x_ref.at[pl.ds(pl.multiple_of(p * 128 + r0, 8), n), :],
            lambda j, k: tx_send.at[j, k],
            lambda j: tx_recv.at[p, j],
        )

    def to_sibling(p):
        return remote(x_ref.at[panel_rows(p)], x_ref.at[panel_rows(p)], sibling, near_send.at[0], near_recv.at[p])

    lax.fori_loop(0, 4, chol_one, 0)

    def receive_panel(p, carry):
        _, arrive, sent = panel_tree(p)
        for s in range(3):
            arrive(s)
        to_sibling(p).start()
        sent()
        to_sibling(p).wait_send()
        return carry

    @pl.when((core == 0) & jnp.logical_not(is_root))
    def _():
        lax.fori_loop(0, 4, receive_panel, 0)

    @pl.when(is_root)
    def _():
        panel_tree(3)[2]()
        to_sibling(3).wait_send()

    @pl.when(core == 1)
    def _():
        for p in range(4):
            to_sibling(p).wait_recv()

    @pl.when(core == 0)
    def _():
        for i, ref in enumerate((a10_ref, a11_ref)):
            remote(ref, ref, sibling, near_send.at[4 + i], near_recv.at[4 + i]).wait_recv()

    @pl.when(jnp.logical_not(self1))
    def _():
        remote(own_ref, own_ref, (1, source_col), sc_send.at[0], sc_recv.at[1]).wait_recv()

    local(r0_ref.at[y, x], blk_ref)
    lower10 = dot_nt(a10_ref[...], x_ref[...])
    own_ref[...] = own_ref[...] - dot(lower10, dot(x_ref[...], blk_ref[...]))
    s11 = a11_ref[...] - dot_nt(lower10, lower10)

    def to_sib(ref, i):
        return remote(ref, ref, sibling, sib_send.at[i], sib_recv.at[i])

    def own_part(r0, n):
        return own_ref.at[pl.ds(r0, n), :]

    send, forward, finish, sent, pair_views = gather(
        PARTS3,
        lambda at, r0, n, c: g_ref.at[at["z"], at["y"], at["x"], c, pl.ds(r0, n), :],
        own_part, ag_send, ag_recv, to_sib,
    )
    send(0)
    local(own_ref, g_ref.at[z, y, x, core])
    for i, (r0, n, h, order) in enumerate(PARTS3):
        to_sib(g_ref.at[z, y, x, core, pl.ds(r0, n), :], i).start()
    s_ref[...] = s11
    unit(x11_ref)
    row_finish(1)

    home_z, home_core = (col % 8) // 2, col % 2
    in_line = core == home_core
    up = (z - home_z + 4) % 4

    def line_copy(m, h):
        src = r0_ref.at[2 * m + col // 8] if h == 0 else c0_ref.at[m]
        return remote(src, c0_ref.at[m], along("z", 1 if m == 0 else 3), c_send.at[m], c_recv.at[m])

    def line_hop(h):
        for m in range(2):
            place = up if m == 0 else (4 - up) % 4

            @pl.when(in_line & (place == h + 1))
            def _(m=m):
                if h >= 0:
                    line_copy(m, 1).wait_recv()
                if h < 2:
                    line_copy(m, h + 1).start()
                src = r0_ref.at[2 * m + col // 8] if h < 0 else c0_ref.at[m]
                remote(src, c0_ref.at[m], sibling, c_send.at[2 + m], c_recv.at[2 + m]).start()

    line_hop(-1)

    @pl.when(in_line & (up == 0))
    def _():
        for m in range(2):
            local(r0_ref.at[2 * m + col // 8], tile_ref)
            local(tile_ref, c0_ref.at[m])

    forward(0)
    finish(0)
    send(1)

    def chol_two(p, carry):
        factor_panel(p, s_ref, x11_ref, u11_ref)

        @pl.when(p == 1)
        def _():
            forward(1)

        @pl.when(p == 2)
        def _():
            finish(1)
            send(2)
            line_hop(0)

        return carry

    lax.fori_loop(0, 4, chol_two, 0)
    line_hop(1)
    forward(2)
    line_hop(2)
    finish(2)

    x00_out[...] = x_ref[...]
    x11_out[...] = x11_ref[...]
    u00_out[...] = u_ref[...]
    u11_out[...] = u11_ref[...]

    sent()
    row_sent()
    for i, v in enumerate(pair_views(core)):
        to_sib(v, i).wait_send()
    for i, v in enumerate(pair_views(1 - core)):
        to_sib(v, i).wait_recv()

    @pl.when(core == 1)
    def _():
        for t in tile_trees:
            t[2]()
        for i, ref in enumerate((a10_ref, a11_ref)):
            remote(ref, ref, sibling, near_send.at[4 + i], near_recv.at[4 + i]).wait_send()

    for m in range(2):
        place = up if m == 0 else (4 - up) % 4

        @pl.when(in_line)
        def _(m=m):
            pl.when(place < 3)(lambda: line_copy(m, 1).wait_send())
            remote(c0_ref.at[m], c0_ref.at[m], sibling, c_send.at[2 + m], c_recv.at[2 + m]).wait_send()

        @pl.when(jnp.logical_not(in_line))
        def _(m=m):
            remote(c0_ref.at[m], c0_ref.at[m], sibling, c_send.at[2 + m], c_recv.at[2 + m]).wait_recv()

    @pl.when(is_source)
    def _():
        for m in range(2):
            for q in range(4):
                c = scatter_copy(m, q, own_ref, sc_recv.at[1])
                pl.when(jnp.logical_not(is_self(m, q)))(c.wait_send)


def split(v):
    high = v.astype(BF16)
    return high, (v - high.astype(F32)).astype(BF16)


def dot16(a, b):
    return lax.dot_general(a, b, (((1,), (0,)), ((), ())), preferred_element_type=F32)


def dot3(a_high, a_low, b_high, b_low):
    return dot16(a_high, b_high) + dot16(a_high, b_low) + dot16(a_low, b_high)


def finish_kernel(
    plan_ref, cov_ref, g_ref, r0_ref, c0_ref, x00_ref, x11_ref, u00_ref, u11_ref,
    f_ref, o_ref,
    xh_ref, xl_ref, row_buf, col_buf, tile_buf, left_ref, right_ref, half_buf, out_buf, zero_buf,
    row_sem, col_sem, tile_sem, f_sem, half_sem, o_sem,
):
    row = lax.axis_index("row")
    col = lax.axis_index("col")

    def panel_tile(i):
        return g_ref.at[(i % 8) // 2, i // 8, :, i % 2]

    def row_copy(l, k):
        src = r0_ref.at[l] if k == 0 else panel_tile(l * 8 + row)
        return pltpu.make_async_copy(src, row_buf.at[k, l], row_sem.at[k, l])

    def col_copy(m, k):
        src = c0_ref.at[m] if k == 0 else panel_tile(m * 16 + col)
        return pltpu.make_async_copy(src, col_buf.at[k, m], col_sem.at[k, m])

    def tile_copy(n):
        return pltpu.make_async_copy(cov_ref.at[n // 2, n % 2], tile_buf.at[n], tile_sem.at[n])

    def f_copy(n):
        return pltpu.make_async_copy(tile_buf.at[n], f_ref.at[n // 2, n % 2], f_sem.at[n])

    def place(n):
        return (n // 2) * 8 + row, (n % 2) * 16 + col

    def updated(n):
        i, j = place(n)
        return (j > 1) & (i >= j)

    def entry(s):
        t = plan_ref[s]
        u = jnp.maximum(t, 0)
        return t >= 0, u // 4, (u // 2) % 2, u % 2

    def half_copy(s):
        _, _, m, h = entry(s)
        j = m * 16 + s
        src = g_ref.at[(j % 8) // 2, j // 8, pl.ds(2 * h, 2), j % 2]
        return pltpu.make_async_copy(src, half_buf.at[s % 2], half_sem.at[s % 2])

    for m in range(2):
        for k in range(2):
            col_copy(m, k).start()
    for l in range(4):
        for k in range(2):
            row_copy(l, k).start()
    for n in range(8):
        pl.when(updated(n))(tile_copy(n).start)
    pl.when(entry(0)[0])(lambda: half_copy(0).start())

    for k, ref in enumerate((x00_ref, x11_ref)):
        xh_ref[k], xl_ref[k] = split(ref[...])
    zero_buf[...] = jnp.zeros((NB, HALF), F32)

    def solved(k, blocks):
        bh, bl = split(jnp.concatenate(blocks, 1))
        return dot3(xh_ref[k], xl_ref[k], bh, bl)

    def make_col(m, carry):
        for k in range(2):
            col_copy(m, k).wait()
            h, low = split(solved(k, [col_buf[k, m, q] for q in range(4)]))
            right_ref[m, k * NB : (k + 1) * NB, :] = h
            right_ref[m, (2 + k) * NB : (3 + k) * NB, :] = low
        return carry

    lax.fori_loop(0, 2, make_col, 0)

    def make_row(l, carry):
        for k in range(2):
            row_copy(l, k).wait()
            p = solved(k, [row_buf[k, l, q] for q in range(4)]).T
            h, low = split(p)
            left_ref[l, :, k * NB : (k + 1) * NB] = h
            left_ref[l, :, (2 + k) * NB : (3 + k) * NB] = low
            i = l * 8 + row

            @pl.when(col == k)
            def _():
                tile_buf[2 * l] = p

                @pl.when(i == k)
                def _():
                    tile_buf[2 * l] = (u00_ref if k == 0 else u11_ref)[...].T

                @pl.when(i < k)
                def _():
                    tile_buf[2 * l] = jnp.zeros((NB, NB), F32)

        return carry

    lax.fori_loop(0, 4, make_row, 0)

    def trailing(n, carry):
        i, j = place(n)
        l, m = n // 2, n % 2

        @pl.when(updated(n))
        def _():
            tile_copy(n).wait()
            tile_buf[n] = tile_buf[n] - dot3(
                left_ref[l, :, : 2 * NB], left_ref[l, :, 2 * NB :],
                right_ref[m, : 2 * NB, :], right_ref[m, 2 * NB :, :],
            )

        @pl.when((j > 1) & (i < j))
        def _():
            tile_buf[n] = jnp.zeros((NB, NB), F32)

        f_copy(n).start()
        return carry

    lax.fori_loop(0, 8, trailing, 0)

    def out_copy(s):
        return pltpu.make_async_copy(out_buf.at[s % 2], o_ref.at[s], o_sem.at[s % 2])

    def moved(s, carry):
        live, l, m, h = entry(s)

        @pl.when(s >= 2)
        def _():
            out_copy(s).wait()

        @pl.when((s < 15) & entry(jnp.minimum(s + 1, 15))[0])
        def _():
            half_copy(jnp.minimum(s + 1, 15)).start()

        @pl.when(live)
        def _():
            half_copy(s).wait()
            bh, bl = split(solved(1, [half_buf[s % 2, q] for q in range(2)]))
            out_buf[s % 2] = dot3(left_ref[l, :, NB : 2 * NB], left_ref[l, :, 3 * NB :], bh, bl)
            out_copy(s).start()

        @pl.when(jnp.logical_not(live))
        def _():
            pltpu.make_async_copy(zero_buf, o_ref.at[s], o_sem.at[s % 2]).start()

        return carry

    lax.fori_loop(0, 16, moved, 0)
    for s in (14, 15):
        out_copy(s).wait()
    for n in range(8):
        f_copy(n).wait()


def per_device(covariance, migration):
    cov = covariance.reshape(4, 2, NB, NB)
    row = lax.axis_index("row")
    col = lax.axis_index("col")
    plan = lax.dynamic_slice(migration, (row, 0, col), (1, 16, 1)).reshape(16)
    dma = pltpu.SemaphoreType.DMA
    square = jax.ShapeDtypeStruct((NB, NB), F32)
    g, r0, c0, x00, x11, u00, u11 = pl.pallas_call(
        exchange_kernel,
        out_shape=[
            jax.ShapeDtypeStruct((4, 4, 4, 2, NB, QB), F32),
            jax.ShapeDtypeStruct((4, 4, NB, QB), F32),
            jax.ShapeDtypeStruct((2, 4, NB, QB), F32),
            square, square, square, square,
        ],
        in_specs=[ANY],
        out_specs=[ANY] * 3 + [VMEM] * 4,
        scratch_shapes=[pltpu.VMEM((NB, NB), F32)] * 7
        + [pltpu.VMEM((NB, QB), F32)] * 2
        + [pltpu.VMEM((4, NB, QB), F32)]
        + [
            dma, dma((8,)), dma((2,)), dma((3, 9)), dma((4, 3)), dma((2, 3, 9)), dma((2, 3)),
            dma((16,)), dma((16,)), dma((36,)), dma((36,)), dma((30,)), dma((30,)),
            dma((4,)), dma((4,)), dma((6,)), dma((6,)),
        ],
        compiler_params=pltpu.CompilerParams(
            collective_id=0, has_side_effects=True, vmem_limit_bytes=48 * 2**20
        ),
        name="exchange",
    )(cov)
    factor, offloaded = pl.pallas_call(
        finish_kernel,
        out_shape=[
            jax.ShapeDtypeStruct((4, 2, NB, NB), F32),
            jax.ShapeDtypeStruct((16, NB, HALF), F32),
        ],
        in_specs=[SMEM] + [ANY] * 4 + [VMEM] * 4,
        out_specs=[ANY, ANY],
        scratch_shapes=[
            pltpu.VMEM((2, NB, NB), BF16), pltpu.VMEM((2, NB, NB), BF16),
            pltpu.VMEM((2, 4, 4, NB, QB), F32), pltpu.VMEM((2, 2, 4, NB, QB), F32),
            pltpu.VMEM((8, NB, NB), F32),
            pltpu.VMEM((4, NB, 4 * NB), BF16), pltpu.VMEM((2, 4 * NB, NB), BF16),
            pltpu.VMEM((2, 2, NB, QB), F32), pltpu.VMEM((2, NB, HALF), F32), pltpu.VMEM((NB, HALF), F32),
            dma((2, 4)), dma((2, 2)), dma((8,)), dma((8,)), dma((2,)), dma((2,)),
        ],
        compiler_params=pltpu.CompilerParams(vmem_limit_bytes=60 * 2**20),
        name="finish",
    )(plan, cov, g, r0, c0, x00, x11, u00, u11)
    return factor[:, None, :, None], offloaded[None, None]


def solution(mesh):
    return jax.shard_map(
        per_device,
        mesh=mesh,
        in_specs=(P(None, "row", None, "col", None, None), P()),
        out_specs=(P(None, "row", None, "col", None, None), P("row", "col", None, None, None)),
        check_vma=False,
    )
```

```python
import functools

import jax
import jax.numpy as jnp
from jax import lax
from jax.experimental import pallas as pl
from jax.experimental.pallas import tpu as pltpu
from jax.sharding import PartitionSpec as P

NB = 512
QB = 128
HALF = 256
MESH = pl.DeviceIdType.MESH
EXACT = lax.Precision.HIGHEST
F32 = jnp.float32
BF16 = jnp.bfloat16
ANY = pl.BlockSpec(memory_space=pl.ANY)
VMEM = pl.BlockSpec(memory_space=pltpu.VMEM)
SMEM = pl.BlockSpec(memory_space=pltpu.SMEM)

PARTS3 = ((0, 176, 88, "xyz"), (176, 168, 88, "yzx"), (344, 168, 88, "zxy"))
PARTS2 = ((0, 256, 128, "xy"), (256, 256, 128, "yx"))
TREE_BLOCK = ((0, 256, "xy"), (256, 256, "yx"))
TREE_PANEL = ((0, 48, "xyz"), (48, 40, "yzx"), (88, 40, "zxy"))
AHEAD = 2
SCHEDULE = sorted(((p, s) for p in range(4) for s in range(3)), key=lambda v: 5.5 * v[0] + 6.0 * v[1])


def dot(a, b):
    return lax.dot_general(
        a, b, (((1,), (0,)), ((), ())), precision=EXACT, preferred_element_type=F32
    )


def dot_nt(a, b):
    return lax.dot_general(
        a, b, (((1,), (1,)), ((), ())), precision=EXACT, preferred_element_type=F32
    )


def lane_spread(v, j):
    return jnp.broadcast_to(v[:, j : j + 1], (8, 128))


def row_spread(v, i):
    return jnp.broadcast_to(v[i : i + 1, :], (8, 128))


def factor128(rows):
    n = len(rows)
    lane = lax.broadcasted_iota(jnp.int32, (8, 128), 1)
    sub = lax.broadcasted_iota(jnp.int32, (8, 128), 0)
    s_rows = list(rows)
    e_rows = [jnp.where(lane == sub + 8 * i, 1.0, 0.0).astype(F32) for i in range(n)]
    upper, inverse = [], []
    zero = jnp.zeros((8, 256), F32)
    for k in range(n):
        cols = [lane_spread(s_rows[k], 8 * k + j) for j in range(8)]
        a = [[row_spread(cols[j], i) if i >= j else None for j in range(8)] for i in range(8)]
        s = [row_spread(s_rows[k], j) for j in range(8)]
        e = [row_spread(e_rows[k], j) for j in range(8)]
        r = [None] * 8
        m = [[None] * 8 for _ in range(8)]
        for j in range(0, 8, 2):
            p, b, c = a[j][j], a[j + 1][j], a[j + 1][j + 1]
            r[j] = 1.0 / p
            r[j + 1] = p * (1.0 / (p * c - b * b))
            for i in range(j + 1, 8):
                m[i][j] = a[i][j] * r[j]
            for i in range(j + 1, 8):
                a[i][j + 1] = a[i][j + 1] - m[i][j] * b
            for i in range(j + 2, 8):
                m[i][j + 1] = a[i][j + 1] * r[j + 1]
            for i in range(j + 2, 8):
                for q in range(j + 2, i + 1):
                    a[i][q] = a[i][q] - m[i][j] * a[q][j] - m[i][j + 1] * a[q][j + 1]
        for j in range(8):
            for i in range(j + 1, 8):
                s[i] = s[i] - m[i][j] * s[j]
                e[i] = e[i] - m[i][j] * e[j]
        u = jnp.zeros((8, 128), F32)
        x = u
        for j in range(8):
            scale = lax.rsqrt(a[j][j])
            u = jnp.where(sub == j, s[j] * scale, u)
            x = jnp.where(sub == j, e[j] * scale, x)
        upper.append(jnp.where(lane >= sub + 8 * k, u, 0.0))
        inverse.append(x)
        if k + 1 == n:
            continue
        ws, we = [None] * 8, [None] * 8
        for j in range(7, -1, -1):
            ws[j] = s[j] * r[j]
            we[j] = e[j] * r[j]
            for i in range(j + 1, 8):
                ws[j] = ws[j] - m[i][j] * ws[i]
                we[j] = we[j] - m[i][j] * we[i]
        last = min(n, k + 1 + AHEAD)
        if last < n:
            w, v = u * 0.0, u * 0.0
            for j in range(8):
                w = jnp.where(sub == j, ws[j], w)
                v = jnp.where(sub == j, we[j], v)
            wide = [zero] * k + [jnp.concatenate([w, v], 1)] + [zero] * (n - 1 - k)
            change = dot(jnp.concatenate(s_rows[last:], 0), jnp.concatenate(wide, 0))
        for i in range(k + 1, last):
            c = [lane_spread(s_rows[i], 8 * k + j) for j in range(8)]
            t, v = s_rows[i], e_rows[i]
            for j in range(8):
                t = t - c[j] * ws[j]
                v = v - c[j] * we[j]
            s_rows[i], e_rows[i] = t, v
        for i in range(last, n):
            g = change[8 * (i - last) : 8 * (i - last) + 8]
            s_rows[i] = s_rows[i] - g[:, :128]
            e_rows[i] = e_rows[i] - g[:, 128:]
    return jnp.concatenate(upper, 0), jnp.concatenate(inverse, 0)


def unit(ref):
    row = lax.broadcasted_iota(jnp.int32, (NB, NB), 0)
    col = lax.broadcasted_iota(jnp.int32, (NB, NB), 1)
    ref[...] = jnp.where(row == col, 1.0, 0.0).astype(F32)


def factor_panel(p, s_ref, x_ref, u_ref, b_ref=None, lt_ref=None):
    base = pl.multiple_of(p * 128, 128)
    here = pl.ds(base, 128)
    rows = [s_ref[pl.ds(pl.multiple_of(base + 8 * i, 8), 8), here] for i in range(16)]
    upper, inverse = factor128(rows)
    across = dot(inverse, s_ref[here, :])
    place = lax.broadcasted_iota(jnp.int32, (128, NB), 1)
    u_ref[here, :] = jnp.where(place >= base + 128, across, 0.0)
    u_ref[here, here] = upper
    xrow = dot(inverse, x_ref[here, :])
    x_ref[here, :] = xrow
    if b_ref is not None:
        brow = dot(inverse, b_ref[here, :])
        lt_ref[here, :] = brow

    @pl.when(p < 3)
    def _():
        below = dot_nt(s_ref[:, here], inverse)
        place = lax.broadcasted_iota(jnp.int32, (NB, 128), 0)
        below = jnp.where(place >= base + 128, below, 0.0)
        s_ref[...] = s_ref[...] - dot(below, across)
        x_ref[...] = x_ref[...] - dot(below, xrow)
        if b_ref is not None:
            b_ref[...] = b_ref[...] - dot(below, brow)


def exchange_kernel(
    cov_ref, g_ref, r0_ref, c0_ref, x00_out, x11_out, u00_out, u11_out,
    s_ref, w_ref, u_ref, x11_ref, u11_ref, a10_ref, a11_ref, own_ref, blk_ref,
    local_sem, out_sem, pre_send, pre_recv, tz_send, tz_recv, sc_send, sc_recv, rs_send, tx_send, tx_recv, ts_send, ts_recv, sh_send, sh_recv, ta_send, ta_recv,
    row_send, row_recv, ag_send, ag_recv, sib_send, sib_recv, c_send, c_recv, near_send, near_recv,
):
    row = lax.axis_index("row")
    col = lax.axis_index("col")
    z, core = row // 2, row % 2
    y, x = col // 4, col % 4
    pos = {"x": x, "y": y, "z": z}

    def along(axis, delta):
        q = dict(pos)
        q[axis] = (q[axis] + delta) % 4
        return (q["z"] * 2 + core, q["y"] * 4 + q["x"])

    sibling = (z * 2 + (1 - core), col)

    def remote(src, dst, target, ssem, rsem):
        return pltpu.make_async_remote_copy(
            src_ref=src, dst_ref=dst, send_sem=ssem, recv_sem=rsem, device_id=target, device_id_type=MESH
        )

    def local(src, dst):
        c = pltpu.make_async_copy(src, dst, local_sem)
        c.start()
        c.wait()

    is_root = (row == 0) & (col == 0)
    source_col = (y % 2) * 8 + row
    w_ref[:, NB:] = jnp.zeros((NB, NB), F32)

    barrier = pltpu.get_barrier_semaphore()

    def greet(target):
        pl.semaphore_signal(barrier, inc=1, device_id=target, device_id_type=MESH)

    def spread_target(m, q):
        return (q * 2 + m, col)

    def spread_self(m, q):
        return q * 2 + m == row

    def row_target(m, q):
        l = 2 * m + col // 8
        return (col % 8, l * 4 + q), l

    def row_self(m, q):
        target, _ = row_target(m, q)
        return (target[0] == row) & (target[1] == col)

    for axis in "xyz":
        for delta in (1, 2, 3):
            greet(along(axis, delta))
    greet(sibling)
    for which in range(2):
        pl.when(row != which)(functools.partial(greet, (which, col)))
    pl.when(jnp.logical_not(is_root))(lambda: greet((0, source_col)))

    @pl.when(row < 2)
    def _():
        for m in range(2):
            for q in range(4):
                pl.when(jnp.logical_not(spread_self(m, q)))(functools.partial(greet, spread_target(m, q)))

    @pl.when(row == 0)
    def _():
        for m in range(2):
            for q in range(4):
                pl.when(jnp.logical_not(row_self(m, q)))(functools.partial(greet, row_target(m, q)[0]))

    first = (row == 0).astype(jnp.int32)
    second = (row == 1).astype(jnp.int32)
    root_i = is_root.astype(jnp.int32)
    pl.semaphore_wait(barrier, 10 + (2 - first - second) + (1 - root_i) + 7 * (first + second) + 8 * first - root_i)

    def quarter(m, q):
        return cov_ref.at[0, m, :, pl.ds(128 * q, 128)]

    def spread_copy(m, q, which):
        dst = c0_ref.at[m, q] if which == 0 else own_ref
        return remote(quarter(m, q), dst, spread_target(m, q), sc_send.at[m * 4 + q], sc_recv.at[which])

    def row_copy(m, q):
        target, l = row_target(m, q)
        return remote(quarter(m, q), r0_ref.at[l, q], target, rs_send.at[m * 4 + q], sc_recv.at[2])

    def tile_block(q):
        return a11_ref.at[:, pl.ds(pl.multiple_of(q * 128, 128), 128)]

    def hand_over(q):
        return remote(quarter(0, q), tile_block(q), (2 * q + 1, col), pre_send.at[q], pre_recv)

    def tile_to_root():
        return remote(cov_ref.at[0, 0], a10_ref, sibling, near_send.at[5], near_recv.at[5])

    @pl.when((row == 1) & (col == 0))
    def _():
        tile_to_root().start()

    @pl.when((row == 1) & (col == 1))
    def _():
        for q in range(1, 4):
            hand_over(q).start()

    for which in range(2):

        @pl.when(row == which)
        def _(which=which):
            for m in range(2):
                for q in range(4):
                    pl.when(jnp.logical_not(spread_self(m, q)))(spread_copy(m, q, which).start)

    @pl.when(row == 0)
    def _():
        local(quarter(0, 0), blk_ref)
        local(blk_ref, c0_ref.at[0, 0])

    @pl.when(row == 0)
    def _():
        for m in range(2):
            for q in range(4):
                pl.when(jnp.logical_not(row_self(m, q)))(row_copy(m, q).start)

    @pl.when(is_root)
    def _():
        local(blk_ref, r0_ref.at[0, 0])

    @pl.when(row == 1)
    def _():
        local(quarter(1, 0), own_ref)

    def level(order, root):
        found = -1
        for t, a in enumerate(order):
            found = jnp.where(pos[a] != root[a], t, found)
        return found

    def tree(parts, roots, piece, ssem, rsem):
        levels = [level(order, root) for (_, _, order), root in zip(parts, roots)]
        count = len(parts)
        depth = len(parts[0][2])

        def copy(i, t, k):
            r0, n, order = parts[i]
            return remote(piece(r0, n), piece(r0, n), along(order[t], k + 1), ssem(i, t * 3 + k), rsem(i))

        def begin(chosen=range(len(parts))):
            for t in range(depth):
                for i in chosen:
                    for k in range(3):
                        copy(i, t, k).start()

        def arrive(s):
            for i in range(count):

                @pl.when(levels[i] == s)
                def _(i=i):
                    copy(i, 0, 0).wait_recv()
                    for t in range(s + 1, depth):
                        for k in range(3):
                            copy(i, t, k).start()

        def sent():
            for i in range(count):
                for t in range(depth):

                    @pl.when(levels[i] < t)
                    def _(i=i, t=t):
                        for k in range(3):
                            copy(i, t, k).wait_send()

        return begin, arrive, sent, levels

    zero_root = {"x": 0, "y": 0, "z": 0}

    def panel_piece(p, r0, n):
        return w_ref.at[pl.ds(128 * p + r0, n), pl.ds(NB, 128 * (p + 1))]

    panel_trees = [
        tree(
            TREE_PANEL, [zero_root] * 3, functools.partial(panel_piece, p),
            lambda j, k, p=p: tx_send.at[p, j, k],
            lambda j, p=p: tx_recv.at[p, j],
        )
        for p in range(4)
    ]

    def panel_to_sibling(p):
        ref = panel_piece(p, 0, 128)
        return remote(ref, ref, sibling, near_send.at[p], near_recv.at[p])

    def side_piece(p, r0, n):
        return w_ref.at[pl.ds(128 * p + r0, n), pl.ds(0, NB)]

    side_trees = [
        tree(
            TREE_PANEL, [zero_root] * 3, functools.partial(side_piece, p),
            lambda j, k, p=p: ts_send.at[p, j, k],
            lambda j, p=p: ts_recv.at[p, j],
        )
        for p in range(4)
    ]

    def side_hand(p):
        return remote(
            a10_ref.at[pl.ds(128 * p, 128), :], side_piece(p, 0, 128), sibling, sh_send.at[p], sh_recv.at[p]
        )

    def side_to_sibling(p):
        ref = side_piece(p, 0, 128)
        return remote(ref, ref, sibling, near_send.at[6 + p], near_recv.at[6 + p])

    tile_begin, tile_arrive, tile_sent, _ = tree(
        TREE_BLOCK, [{"x": 1, "y": 0}] * 2,
        lambda r0, n: tile_block(z).at[pl.ds(r0, n), :],
        lambda j, k: ta_send.at[j, k],
        lambda j: ta_recv.at[j],
    )

    def tile_along(k):
        return remote(tile_block(z), tile_block(z), along("z", k + 1), tz_send.at[k], tz_recv.at[k])

    def tile_from(k):
        ref = tile_block((z + 3 - k) % 4)
        return remote(ref, ref, along("z", 3 - k), tz_send.at[k], tz_recv.at[k])

    def tile_to_sibling():
        return remote(a11_ref, a11_ref, sibling, near_send.at[4], near_recv.at[4])

    @pl.when(jnp.logical_not(is_root))
    def _():
        u_ref[...] = jnp.zeros((NB, NB), F32)

    @pl.when(is_root)
    def _():
        local(cov_ref.at[0, 0], s_ref)
        unit(x11_ref)
        tile_to_root().wait_recv()
        u11_ref[...] = a10_ref[...].T

    def gather(parts, view, own, ssem, rsem, sib=None):
        phases = len(parts[0][3])

        def part_view(order, k, delta, r0, n, c=core):
            at = {}
            for j, a in enumerate(order):
                if j < k:
                    at[a] = slice(None)
                elif j == k:
                    at[a] = (pos[a] + delta) % 4
                else:
                    at[a] = pos[a]
            return view(at, r0, n, c)

        def number(k, i):
            return (k * len(parts) + i) * 4

        def direct(k, i, j):
            r0, n, h, order = parts[i]
            m = number(k, i)
            dst = part_view(order, k, 0, r0, n)
            src = own(r0, n) if k == 0 else dst
            return remote(src, dst, along(order[k], (1, 3)[j]), ssem.at[m + j], rsem.at[m + j])

        def passed(k, i, j, back):
            r0, n, h, order = parts[i]
            m = number(k, i) + 2 + j
            q0, qn = ((r0, h), (r0 + h, n - h))[j]
            half = part_view(order, k, back, q0, qn)
            return remote(half, half, along(order[k], (1, 3)[j]), ssem.at[m], rsem.at[m])

        def send(k):
            for i in range(len(parts)):
                for j in range(2):
                    direct(k, i, j).start()

        def forward(k):
            for i, (r0, n, h, order) in enumerate(parts):
                m = number(k, i)
                for j, back in ((0, 3), (1, 1)):
                    got = part_view(order, k, back, r0, n)
                    remote(got, got, along(order[k], 1), ssem.at[m + j], rsem.at[m + j]).wait_recv()
                    passed(k, i, j, back).start()
                    if sib:
                        sib(got, 3 + k * 9 + i * 2 + j).start()

        def finish(k):
            for i, (r0, n, h, order) in enumerate(parts):
                for j in range(2):
                    passed(k, i, j, 2).wait_recv()
                if sib:
                    sib(part_view(order, k, 2, r0, n), 3 + k * 9 + 6 + i).start()

        def sent():
            for k in range(phases):
                for i in range(len(parts)):
                    for j in range(2):
                        direct(k, i, j).wait_send()
                        passed(k, i, j, 2).wait_send()

        def pair_views(c):
            views = [part_view(order, 0, 0, r0, n, c) for (r0, n, h, order) in parts]
            for k in range(phases):
                for r0, n, h, order in parts:
                    views.append(part_view(order, k, 3, r0, n, c))
                    views.append(part_view(order, k, 1, r0, n, c))
                for r0, n, h, order in parts:
                    views.append(part_view(order, k, 2, r0, n, c))
            return views

        return send, forward, finish, sent, pair_views

    row_send_step, row_forward, row_finish, row_sent, _ = gather(
        PARTS2,
        lambda at, r0, n, c: r0_ref.at[at["y"], at["x"], pl.ds(r0, n), :],
        lambda r0, n: r0_ref.at[y, x, pl.ds(r0, n), :],
        row_send, row_recv,
    )

    def row_begin():
        @pl.when(jnp.logical_not(is_root))
        def _():
            remote(r0_ref.at[y, x], r0_ref.at[y, x], (0, source_col), rs_send.at[0], sc_recv.at[2]).wait_recv()

        row_send_step(0)

    def chol_one(p, carry):
        factor_panel(p, s_ref, x11_ref, u_ref, u11_ref, a10_ref)
        here = pl.ds(pl.multiple_of(p * 128, 128), 128)
        w_ref[here, NB:] = x11_ref[here, :]
        for k in range(4):

            @pl.when(p == k)
            def _(k=k):
                side_hand(k).start()
                panel_trees[k][0]()
                panel_to_sibling(k).start()

        return carry

    @pl.when(is_root)
    def _():
        lax.fori_loop(0, 4, chol_one, 0)

    @pl.when((core == 0) & jnp.logical_not(is_root))
    def _():
        for p, s in SCHEDULE:
            panel_trees[p][1](s)
            if s == 2:
                panel_to_sibling(p).start()

    @pl.when(core == 0)
    def _():
        for p in range(4):
            side_to_sibling(p).wait_recv()

    @pl.when(core == 1)
    def _():
        @pl.when(col == 1)
        def _():
            pl.when(row == 1)(lambda: local(quarter(0, 0), tile_block(0)))
            pl.when(row != 1)(lambda: hand_over(z).wait_recv())
            tile_begin()

        is_hand = (row == 1) & (col == 0)

        @pl.when(is_hand)
        def _():
            for s in range(2):
                tile_arrive(s)
            for k in range(3):
                tile_along(k).start()
            for p in range(4):
                side_hand(p).wait_recv()
                side_trees[p][0]()
                side_to_sibling(p).start()

        @pl.when(jnp.logical_not(is_hand))
        def _():
            tile_arrive(0)
            for n, (p, s) in enumerate(SCHEDULE):
                side_trees[p][1](s)
                if s == 2:
                    side_to_sibling(p).start()
                if n == 0:
                    tile_arrive(1)
                    for k in range(3):
                        tile_along(k).start()

        for p in range(4):
            panel_to_sibling(p).wait_recv()

    for which in range(2):

        @pl.when(row != which)
        def _(which=which):
            ref = c0_ref.at[core, z] if which == 0 else own_ref
            remote(ref, ref, (which, col), sc_send.at[0], sc_recv.at[which]).wait_recv()

    local(c0_ref.at[core, z], blk_ref)
    lower10 = w_ref[:, :NB].T
    own_ref[...] = own_ref[...] - dot(lower10, dot(w_ref[:, NB:], blk_ref[...]))

    def to_sib(ref, i):
        return remote(ref, ref, sibling, sib_send.at[i], sib_recv.at[i])

    def own_part(r0, n):
        return own_ref.at[pl.ds(r0, n), :]

    send, forward, finish, sent, pair_views = gather(
        PARTS3,
        lambda at, r0, n, c: g_ref.at[at["z"], at["y"], at["x"], c, pl.ds(r0, n), :],
        own_part, ag_send, ag_recv, to_sib,
    )
    send(0)
    local(own_ref, g_ref.at[z, y, x, core])
    for i, (r0, n, h, order) in enumerate(PARTS3):
        to_sib(g_ref.at[z, y, x, core, pl.ds(r0, n), :], i).start()
    pltpu.make_async_copy(w_ref.at[:, pl.ds(NB, NB)], x00_out, out_sem.at[0]).start()
    def line_copy(k):
        ref = c0_ref.at[core, z]
        return remote(ref, ref, along("z", k + 1), c_send.at[k], c_recv.at[k])

    def line_from(k):
        ref = c0_ref.at[core, (z + 3 - k) % 4]
        return remote(ref, ref, along("z", 3 - k), c_send.at[k], c_recv.at[k])

    def line_to_sibling(m):
        return remote(c0_ref.at[m], c0_ref.at[m], sibling, c_send.at[3], c_recv.at[3])

    forward(0)
    finish(0)
    send(1)
    row_begin()
    for k in range(3):
        line_copy(k).start()
    forward(1)
    row_forward(0)
    finish(1)
    send(2)
    row_finish(0)
    row_send_step(1)

    @pl.when(core == 1)
    def _():
        for k in range(3):
            tile_from(k).wait_recv()
        tile_to_sibling().start()

    pl.when(core == 0)(lambda: tile_to_sibling().wait_recv())
    s_ref[...] = a11_ref[...] - dot(lower10, w_ref[:, :NB])
    unit(x11_ref)

    def chol_two(p, carry):
        factor_panel(p, s_ref, x11_ref, u11_ref)
        return carry

    lax.fori_loop(0, 4, chol_two, 0)
    pltpu.make_async_copy(x11_ref, x11_out, out_sem.at[1]).start()
    pltpu.make_async_copy(u11_ref, u11_out, out_sem.at[2]).start()
    pltpu.make_async_copy(u_ref, u00_out, out_sem.at[3]).start()
    row_forward(1)
    for k in range(3):
        line_from(k).wait_recv()
    line_to_sibling(core).start()
    forward(2)
    row_finish(1)
    finish(2)

    pltpu.make_async_copy(w_ref.at[:, pl.ds(NB, NB)], x00_out, out_sem.at[0]).wait()
    pltpu.make_async_copy(x11_ref, x11_out, out_sem.at[1]).wait()
    pltpu.make_async_copy(u11_ref, u11_out, out_sem.at[2]).wait()
    pltpu.make_async_copy(u_ref, u00_out, out_sem.at[3]).wait()
    sent()
    row_sent()
    for i, v in enumerate(pair_views(core)):
        to_sib(v, i).wait_send()
    for i, v in enumerate(pair_views(1 - core)):
        to_sib(v, i).wait_recv()

    @pl.when(core == 0)
    def _():
        for p in range(4):
            panel_trees[p][2]()
            panel_to_sibling(p).wait_send()

        @pl.when(is_root)
        def _():
            for p in range(4):
                side_hand(p).wait_send()

    @pl.when(core == 1)
    def _():
        for p in range(4):
            side_trees[p][2]()
            side_to_sibling(p).wait_send()
        tile_sent()
        for k in range(3):
            tile_along(k).wait_send()
        tile_to_sibling().wait_send()

        @pl.when((row == 1) & (col == 0))
        def _():
            tile_to_root().wait_send()

        @pl.when((row == 1) & (col == 1))
        def _():
            for q in range(1, 4):
                hand_over(q).wait_send()

    for k in range(3):
        line_copy(k).wait_send()
    line_to_sibling(core).wait_send()
    line_to_sibling(1 - core).wait_recv()

    @pl.when(row < 2)
    def _():
        for m in range(2):
            for q in range(4):
                pl.when(jnp.logical_not(spread_self(m, q)))(spread_copy(m, q, 1).wait_send)

    @pl.when(row == 0)
    def _():
        for m in range(2):
            for q in range(4):
                pl.when(jnp.logical_not(row_self(m, q)))(row_copy(m, q).wait_send)


def split(v):
    high = v.astype(BF16)
    return high, (v - high.astype(F32)).astype(BF16)


def dot16(a, b):
    return lax.dot_general(a, b, (((1,), (0,)), ((), ())), preferred_element_type=F32)


def left_parts(v):
    high, low = split(v)
    return jnp.concatenate([high, high, low], 1)


def right_parts(v):
    high, low = split(v)
    return jnp.concatenate([high, low, high], 0)


def finish_kernel(
    plan_ref, cov_ref, g_ref, r0_ref, c0_ref, x00_ref, x11_ref, u00_ref, u11_ref,
    f_ref, o_ref,
    x_buf, xt_ref, xb_ref, row_buf, col_buf, tile_buf, left_ref, right_ref, half_buf, out_buf, zero_buf,
    x_sem, row_sem, col_sem, tile_sem, f_sem, half_sem, o_sem,
):
    row = lax.axis_index("row")
    col = lax.axis_index("col")

    def panel_tile(i):
        return g_ref.at[:, (i % 16) // 4, i % 4, i // 16]

    def row_copy(l, k):
        src = r0_ref.at[l] if k == 0 else panel_tile(l * 8 + row)
        return pltpu.make_async_copy(src, row_buf.at[k, l], row_sem.at[k, l])

    def col_copy(m, k):
        src = c0_ref.at[m] if k == 0 else panel_tile(m * 16 + col)
        return pltpu.make_async_copy(src, col_buf.at[k, m], col_sem.at[k, m])

    def tile_copy(n):
        return pltpu.make_async_copy(cov_ref.at[n // 2, n % 2], tile_buf.at[n], tile_sem.at[n])

    def f_copy(n):
        return pltpu.make_async_copy(tile_buf.at[n], f_ref.at[n // 2, n % 2], f_sem.at[n])

    def place(n):
        return (n // 2) * 8 + row, (n % 2) * 16 + col

    def updated(n):
        i, j = place(n)
        return (j > 1) & (i >= j)

    def entry(s):
        t = plan_ref[s]
        u = jnp.maximum(t, 0)
        return t >= 0, u // 4, (u // 2) % 2, u % 2

    def half_copy(s):
        _, _, m, h = entry(s)
        src = g_ref.at[pl.ds(2 * h, 2), s // 4, s % 4, m]
        return pltpu.make_async_copy(src, half_buf.at[s % 2], half_sem.at[s % 2])

    def x_copy(k):
        return pltpu.make_async_copy((x00_ref, x11_ref)[k], x_buf.at[k], x_sem.at[k])

    for k in range(2):
        x_copy(k).start()
    for m in range(2):
        for k in range(2):
            col_copy(m, k).start()
    for l in range(4):
        for k in range(2):
            row_copy(l, k).start()
    for n in range(8):
        pl.when(updated(n))(tile_copy(n).start)
    pl.when(entry(0)[0])(lambda: half_copy(0).start())

    for k in range(2):
        x_copy(k).wait()
        xt_ref[k] = left_parts(x_buf[k, :HALF, :HALF])
        xb_ref[k] = left_parts(x_buf[k, HALF:, :])
    zero_buf[...] = jnp.zeros((NB, HALF), F32)

    def solved(k, blocks):
        tile = jnp.concatenate(blocks, 1)
        top = dot16(xt_ref[k], right_parts(tile[:HALF]))
        return jnp.concatenate([top, dot16(xb_ref[k], right_parts(tile))], 0)

    def make_col(m, carry):
        for k in range(2):
            col_copy(m, k).wait()
            right_ref[m, 3 * k * NB : 3 * (k + 1) * NB, :] = right_parts(
                solved(k, [col_buf[k, m, q] for q in range(4)])
            )
        return carry

    lax.fori_loop(0, 2, make_col, 0)

    def make_row(l, carry):
        for k in range(2):
            row_copy(l, k).wait()
            p = solved(k, [row_buf[k, l, q] for q in range(4)]).T
            left_ref[l, :, 3 * k * NB : 3 * (k + 1) * NB] = left_parts(p)
            i = l * 8 + row

            @pl.when(col == k)
            def _():
                tile_buf[2 * l] = p

                @pl.when(i == k)
                def _():
                    factor = pltpu.make_async_copy((u00_ref, u11_ref)[k], x_buf.at[k], x_sem.at[k])
                    factor.start()
                    factor.wait()
                    tile_buf[2 * l] = x_buf[k].T

                @pl.when(i < k)
                def _():
                    tile_buf[2 * l] = jnp.zeros((NB, NB), F32)

        return carry

    lax.fori_loop(0, 4, make_row, 0)

    def trailing(n, carry):
        i, j = place(n)
        l, m = n // 2, n % 2

        @pl.when(updated(n))
        def _():
            tile_copy(n).wait()
            tile_buf[n] = tile_buf[n] - dot16(left_ref[l], right_ref[m])

        @pl.when((j > 1) & (i < j))
        def _():
            tile_buf[n] = jnp.zeros((NB, NB), F32)

        f_copy(n).start()
        return carry

    lax.fori_loop(0, 8, trailing, 0)

    def out_copy(s):
        return pltpu.make_async_copy(out_buf.at[s % 2], o_ref.at[s], o_sem.at[s % 2])

    def moved(s, carry):
        live, l, m, h = entry(s)

        @pl.when(s >= 2)
        def _():
            out_copy(s).wait()

        @pl.when((s < 15) & entry(jnp.minimum(s + 1, 15))[0])
        def _():
            half_copy(jnp.minimum(s + 1, 15)).start()

        @pl.when(live)
        def _():
            half_copy(s).wait()
            right = right_parts(solved(1, [half_buf[s % 2, q] for q in range(2)]))
            out_buf[s % 2] = dot16(left_ref[l, :, 3 * NB :], right)
            out_copy(s).start()

        @pl.when(jnp.logical_not(live))
        def _():
            pltpu.make_async_copy(zero_buf, o_ref.at[s], o_sem.at[s % 2]).start()

        return carry

    lax.fori_loop(0, 16, moved, 0)
    for s in (14, 15):
        out_copy(s).wait()
    for n in range(8):
        f_copy(n).wait()


def per_device(covariance, migration):
    cov = covariance.reshape(4, 2, NB, NB)
    row = lax.axis_index("row")
    col = lax.axis_index("col")
    plan = lax.dynamic_slice(migration, (row, 0, col), (1, 16, 1)).reshape(16)
    dma = pltpu.SemaphoreType.DMA
    square = jax.ShapeDtypeStruct((NB, NB), F32)
    g, r0, c0, x00, x11, u00, u11 = pl.pallas_call(
        exchange_kernel,
        out_shape=[
            jax.ShapeDtypeStruct((4, 4, 4, 2, NB, QB), F32),
            jax.ShapeDtypeStruct((4, 4, NB, QB), F32),
            jax.ShapeDtypeStruct((2, 4, NB, QB), F32),
            square, square, square, square,
        ],
        in_specs=[ANY],
        out_specs=[ANY] * 7,
        scratch_shapes=[pltpu.VMEM((NB, NB), F32), pltpu.VMEM((NB, 2 * NB), F32)]
        + [pltpu.VMEM((NB, NB), F32)] * 5
        + [pltpu.VMEM((NB, QB), F32)] * 2
        + [
            dma, dma((4,)), dma((4,)), dma, dma((3,)), dma((3,)), dma((8,)), dma((3,)), dma((8,)),
            dma((4, 3, 9)), dma((4, 3)), dma((4, 3, 9)), dma((4, 3)), dma((4,)), dma((4,)), dma((2, 6)), dma((2,)),
            dma((16,)), dma((16,)), dma((36,)), dma((36,)), dma((30,)), dma((30,)),
            dma((4,)), dma((4,)), dma((10,)), dma((10,)),
        ],
        compiler_params=pltpu.CompilerParams(
            collective_id=0, has_side_effects=True, vmem_limit_bytes=48 * 2**20
        ),
        name="exchange",
    )(cov)
    factor, offloaded = pl.pallas_call(
        finish_kernel,
        out_shape=[
            jax.ShapeDtypeStruct((4, 2, NB, NB), F32),
            jax.ShapeDtypeStruct((16, NB, HALF), F32),
        ],
        in_specs=[SMEM] + [ANY] * 8,
        out_specs=[ANY, ANY],
        scratch_shapes=[
            pltpu.VMEM((2, NB, NB), F32), pltpu.VMEM((2, HALF, 3 * HALF), BF16), pltpu.VMEM((2, HALF, 3 * NB), BF16),
            pltpu.VMEM((2, 4, 4, NB, QB), F32), pltpu.VMEM((2, 2, 4, NB, QB), F32),
            pltpu.VMEM((8, NB, NB), F32),
            pltpu.VMEM((4, NB, 6 * NB), BF16), pltpu.VMEM((2, 6 * NB, NB), BF16),
            pltpu.VMEM((2, 2, NB, QB), F32), pltpu.VMEM((2, NB, HALF), F32), pltpu.VMEM((NB, HALF), F32),
            dma((2,)), dma((2, 4)), dma((2, 2)), dma((8,)), dma((8,)), dma((2,)), dma((2,)),
        ],
        compiler_params=pltpu.CompilerParams(vmem_limit_bytes=60 * 2**20),
        name="finish",
    )(plan, cov, g, r0, c0, x00, x11, u00, u11)
    return factor[:, None, :, None], offloaded[None, None]


def solution(mesh):
    return jax.shard_map(
        per_device,
        mesh=mesh,
        in_specs=(P(None, "row", None, "col", None, None), P()),
        out_specs=(P(None, "row", None, "col", None, None), P("row", "col", None, None, None)),
        check_vma=False,
    )
```

```python
import functools

import jax
import jax.numpy as jnp
from jax import lax
from jax.experimental import pallas as pl
from jax.experimental.pallas import tpu as pltpu
from jax.sharding import PartitionSpec as P

NB = 512
QB = 128
HALF = 256
MESH = pl.DeviceIdType.MESH
EXACT = lax.Precision.HIGHEST
F32 = jnp.float32
BF16 = jnp.bfloat16
ANY = pl.BlockSpec(memory_space=pl.ANY)
VMEM = pl.BlockSpec(memory_space=pltpu.VMEM)
SMEM = pl.BlockSpec(memory_space=pltpu.SMEM)

PARTS3 = ((0, 176, 88, "xyz"), (176, 168, 88, "yzx"), (344, 168, 88, "zxy"))
PARTS2 = ((0, 256, 128, "xy"), (256, 256, 128, "yx"))
TREE_BLOCK = ((0, 256, "xy"), (256, 256, "yx"))
TREE_PANEL = ((0, 48, "xyz"), (48, 40, "yzx"), (88, 40, "zxy"))
AHEAD = 2


def dot(a, b):
    return lax.dot_general(
        a, b, (((1,), (0,)), ((), ())), precision=EXACT, preferred_element_type=F32
    )


def dot_nt(a, b):
    return lax.dot_general(
        a, b, (((1,), (1,)), ((), ())), precision=EXACT, preferred_element_type=F32
    )


def lane_spread(v, j):
    return jnp.broadcast_to(v[:, j : j + 1], (8, 128))


def row_spread(v, i):
    return jnp.broadcast_to(v[i : i + 1, :], (8, 128))


def factor128(rows):
    n = len(rows)
    lane = lax.broadcasted_iota(jnp.int32, (8, 128), 1)
    sub = lax.broadcasted_iota(jnp.int32, (8, 128), 0)
    s_rows = list(rows)
    e_rows = [jnp.where(lane == sub + 8 * i, 1.0, 0.0).astype(F32) for i in range(n)]
    upper, inverse = [], []
    zero = jnp.zeros((8, 256), F32)
    for k in range(n):
        cols = [lane_spread(s_rows[k], 8 * k + j) for j in range(8)]
        a = [[row_spread(cols[j], i) if i >= j else None for j in range(8)] for i in range(8)]
        s = [row_spread(s_rows[k], j) for j in range(8)]
        e = [row_spread(e_rows[k], j) for j in range(8)]
        r = [None] * 8
        m = [[None] * 8 for _ in range(8)]
        for j in range(0, 8, 2):
            p, b, c = a[j][j], a[j + 1][j], a[j + 1][j + 1]
            r[j] = 1.0 / p
            r[j + 1] = p * (1.0 / (p * c - b * b))
            for i in range(j + 1, 8):
                m[i][j] = a[i][j] * r[j]
            for i in range(j + 1, 8):
                a[i][j + 1] = a[i][j + 1] - m[i][j] * b
            for i in range(j + 2, 8):
                m[i][j + 1] = a[i][j + 1] * r[j + 1]
            for i in range(j + 2, 8):
                for q in range(j + 2, i + 1):
                    a[i][q] = a[i][q] - m[i][j] * a[q][j] - m[i][j + 1] * a[q][j + 1]
        for j in range(8):
            for i in range(j + 1, 8):
                s[i] = s[i] - m[i][j] * s[j]
                e[i] = e[i] - m[i][j] * e[j]
        u = jnp.zeros((8, 128), F32)
        x = u
        for j in range(8):
            scale = lax.rsqrt(a[j][j])
            u = jnp.where(sub == j, s[j] * scale, u)
            x = jnp.where(sub == j, e[j] * scale, x)
        upper.append(jnp.where(lane >= sub + 8 * k, u, 0.0))
        inverse.append(x)
        if k + 1 == n:
            continue
        ws, we = [None] * 8, [None] * 8
        for j in range(7, -1, -1):
            ws[j] = s[j] * r[j]
            we[j] = e[j] * r[j]
            for i in range(j + 1, 8):
                ws[j] = ws[j] - m[i][j] * ws[i]
                we[j] = we[j] - m[i][j] * we[i]
        last = min(n, k + 1 + AHEAD)
        if last < n:
            w, v = u * 0.0, u * 0.0
            for j in range(8):
                w = jnp.where(sub == j, ws[j], w)
                v = jnp.where(sub == j, we[j], v)
            wide = [zero] * k + [jnp.concatenate([w, v], 1)] + [zero] * (n - 1 - k)
            change = dot(jnp.concatenate(s_rows[last:], 0), jnp.concatenate(wide, 0))
        for i in range(k + 1, last):
            c = [lane_spread(s_rows[i], 8 * k + j) for j in range(8)]
            t, v = s_rows[i], e_rows[i]
            for j in range(8):
                t = t - c[j] * ws[j]
                v = v - c[j] * we[j]
            s_rows[i], e_rows[i] = t, v
        for i in range(last, n):
            g = change[8 * (i - last) : 8 * (i - last) + 8]
            s_rows[i] = s_rows[i] - g[:, :128]
            e_rows[i] = e_rows[i] - g[:, 128:]
    return jnp.concatenate(upper, 0), jnp.concatenate(inverse, 0)


def unit(ref):
    row = lax.broadcasted_iota(jnp.int32, (NB, NB), 0)
    col = lax.broadcasted_iota(jnp.int32, (NB, NB), 1)
    ref[...] = jnp.where(row == col, 1.0, 0.0).astype(F32)


def factor_panel(p, s_ref, x_ref, u_ref):
    base = pl.multiple_of(p * 128, 128)
    here = pl.ds(base, 128)
    rows = [s_ref[pl.ds(pl.multiple_of(base + 8 * i, 8), 8), here] for i in range(16)]
    upper, inverse = factor128(rows)
    across = dot(inverse, s_ref[here, :])
    place = lax.broadcasted_iota(jnp.int32, (128, NB), 1)
    u_ref[here, :] = jnp.where(place >= base + 128, across, 0.0)
    u_ref[here, here] = upper
    xrow = dot(inverse, x_ref[here, :])
    x_ref[here, :] = xrow

    @pl.when(p < 3)
    def _():
        below = dot_nt(s_ref[:, here], inverse)
        place = lax.broadcasted_iota(jnp.int32, (NB, 128), 0)
        below = jnp.where(place >= base + 128, below, 0.0)
        s_ref[...] = s_ref[...] - dot(below, across)
        x_ref[...] = x_ref[...] - dot(below, xrow)


def exchange_kernel(
    cov_ref, g_ref, r0_ref, c0_ref, x00_out, x11_out, u00_out, u11_out,
    s_ref, x_ref, u_ref, x11_ref, u11_ref, a10_ref, a11_ref, own_ref, blk_ref,
    local_sem, pre_send, pre_recv, tz_send, tz_recv, sc_send, sc_recv, rs_send, tx_send, tx_recv, ta_send, ta_recv,
    row_send, row_recv, ag_send, ag_recv, sib_send, sib_recv, c_send, c_recv, near_send, near_recv,
):
    row = lax.axis_index("row")
    col = lax.axis_index("col")
    z, core = row // 2, row % 2
    y, x = col // 4, col % 4
    pos = {"x": x, "y": y, "z": z}

    def along(axis, delta):
        q = dict(pos)
        q[axis] = (q[axis] + delta) % 4
        return (q["z"] * 2 + core, q["y"] * 4 + q["x"])

    sibling = (z * 2 + (1 - core), col)

    def remote(src, dst, target, ssem, rsem):
        return pltpu.make_async_remote_copy(
            src_ref=src, dst_ref=dst, send_sem=ssem, recv_sem=rsem, device_id=target, device_id_type=MESH
        )

    def local(src, dst):
        c = pltpu.make_async_copy(src, dst, local_sem)
        c.start()
        c.wait()

    is_root = (row == 0) & (col == 0)
    source_col = (y % 2) * 8 + row
    x_ref[...] = jnp.zeros((NB, NB), F32)

    barrier = pltpu.get_barrier_semaphore()

    def greet(target):
        pl.semaphore_signal(barrier, inc=1, device_id=target, device_id_type=MESH)

    def spread_target(m, q):
        return (q * 2 + m, col)

    def spread_self(m, q):
        return q * 2 + m == row

    def row_target(m, q):
        l = 2 * m + col // 8
        return (col % 8, l * 4 + q), l

    def row_self(m, q):
        target, _ = row_target(m, q)
        return (target[0] == row) & (target[1] == col)

    for axis in "xyz":
        for delta in (1, 2, 3):
            greet(along(axis, delta))
    greet(sibling)
    for which in range(2):
        pl.when(row != which)(functools.partial(greet, (which, col)))
    pl.when(jnp.logical_not(is_root))(lambda: greet((0, source_col)))

    @pl.when(row < 2)
    def _():
        for m in range(2):
            for q in range(4):
                pl.when(jnp.logical_not(spread_self(m, q)))(functools.partial(greet, spread_target(m, q)))

    @pl.when(row == 0)
    def _():
        for m in range(2):
            for q in range(4):
                pl.when(jnp.logical_not(row_self(m, q)))(functools.partial(greet, row_target(m, q)[0]))

    first = (row == 0).astype(jnp.int32)
    second = (row == 1).astype(jnp.int32)
    root_i = is_root.astype(jnp.int32)
    pl.semaphore_wait(barrier, 10 + (2 - first - second) + (1 - root_i) + 7 * (first + second) + 8 * first - root_i)

    def quarter(m, q):
        return cov_ref.at[0, m, :, pl.ds(128 * q, 128)]

    def spread_copy(m, q, which):
        dst = c0_ref.at[m, q] if which == 0 else own_ref
        return remote(quarter(m, q), dst, spread_target(m, q), sc_send.at[m * 4 + q], sc_recv.at[which])

    def row_copy(m, q):
        target, l = row_target(m, q)
        return remote(quarter(m, q), r0_ref.at[l, q], target, rs_send.at[m * 4 + q], sc_recv.at[2])

    def tile_block(i, q):
        return (a10_ref, a11_ref)[i].at[:, pl.ds(pl.multiple_of(q * 128, 128), 128)]

    def hand_over(i, q):
        return remote(quarter(0, q), tile_block(i, q), (2 * q + 1, col), pre_send.at[q], pre_recv.at[i])

    for i in range(2):

        @pl.when((row == 1) & (col == i))
        def _(i=i):
            for q in range(1, 4):
                hand_over(i, q).start()

    for which in range(2):

        @pl.when(row == which)
        def _(which=which):
            for m in range(2):
                for q in range(4):
                    pl.when(jnp.logical_not(spread_self(m, q)))(spread_copy(m, q, which).start)

    @pl.when(row == 0)
    def _():
        for m in range(2):
            for q in range(4):
                pl.when(jnp.logical_not(row_self(m, q)))(row_copy(m, q).start)
        local(quarter(0, 0), blk_ref)
        local(blk_ref, c0_ref.at[0, 0])

    @pl.when(is_root)
    def _():
        local(blk_ref, r0_ref.at[0, 0])

    @pl.when(row == 1)
    def _():
        local(quarter(1, 0), own_ref)

    def level(order, root):
        found = -1
        for t, a in enumerate(order):
            found = jnp.where(pos[a] != root[a], t, found)
        return found

    def tree(parts, roots, piece, ssem, rsem):
        levels = [level(order, root) for (_, _, order), root in zip(parts, roots)]
        count = len(parts)
        depth = len(parts[0][2])

        def copy(i, t, k):
            r0, n, order = parts[i]
            return remote(piece(r0, n), piece(r0, n), along(order[t], k + 1), ssem(i, t * 3 + k), rsem(i))

        def begin():
            for t in range(depth):
                for i in range(count):
                    for k in range(3):
                        copy(i, t, k).start()

        def arrive(s):
            for i in range(count):

                @pl.when(levels[i] == s)
                def _(i=i):
                    copy(i, 0, 0).wait_recv()
                    for t in range(s + 1, depth):
                        for k in range(3):
                            copy(i, t, k).start()

        def sent():
            for i in range(count):
                for t in range(depth):

                    @pl.when(levels[i] < t)
                    def _(i=i, t=t):
                        for k in range(3):
                            copy(i, t, k).wait_send()

        return begin, arrive, sent, levels

    zero_root = {"x": 0, "y": 0, "z": 0}

    def panel_piece(p, r0, n):
        return x_ref.at[pl.ds(128 * p + r0, n), pl.ds(0, 128 * (p + 1))]

    panel_trees = [
        tree(
            TREE_PANEL, [zero_root] * 3, functools.partial(panel_piece, p),
            lambda j, k, p=p: tx_send.at[p, j, k],
            lambda j, p=p: tx_recv.at[p, j],
        )
        for p in range(4)
    ]

    def panel_to_sibling(p):
        ref = panel_piece(p, 0, 128)
        return remote(ref, ref, sibling, near_send.at[p], near_recv.at[p])

    tile_trees = [
        tree(
            TREE_BLOCK, [{"x": i, "y": 0}] * 2,
            lambda r0, n, i=i: tile_block(i, z).at[pl.ds(r0, n), :],
            lambda j, k, i=i: ta_send.at[i, j, k],
            lambda j, i=i: ta_recv.at[i, j],
        )
        for i in range(2)
    ]

    def tile_along(i, k):
        return remote(tile_block(i, z), tile_block(i, z), along("z", k + 1), tz_send.at[i, k], tz_recv.at[i, k])

    def tile_from(i, k):
        ref = tile_block(i, (z + 3 - k) % 4)
        return remote(ref, ref, along("z", 3 - k), tz_send.at[i, k], tz_recv.at[i, k])

    def tile_to_sibling(i):
        ref = (a10_ref, a11_ref)[i]
        return remote(ref, ref, sibling, near_send.at[4 + i], near_recv.at[4 + i])

    @pl.when(is_root)
    def _():
        local(cov_ref.at[0, 0], s_ref)
        unit(x11_ref)

    def gather(parts, view, own, ssem, rsem, sib=None):
        phases = len(parts[0][3])

        def part_view(order, k, delta, r0, n, c=core):
            at = {}
            for j, a in enumerate(order):
                if j < k:
                    at[a] = slice(None)
                elif j == k:
                    at[a] = (pos[a] + delta) % 4
                else:
                    at[a] = pos[a]
            return view(at, r0, n, c)

        def number(k, i):
            return (k * len(parts) + i) * 4

        def direct(k, i, j):
            r0, n, h, order = parts[i]
            m = number(k, i)
            dst = part_view(order, k, 0, r0, n)
            src = own(r0, n) if k == 0 else dst
            return remote(src, dst, along(order[k], (1, 3)[j]), ssem.at[m + j], rsem.at[m + j])

        def passed(k, i, j, back):
            r0, n, h, order = parts[i]
            m = number(k, i) + 2 + j
            q0, qn = ((r0, h), (r0 + h, n - h))[j]
            half = part_view(order, k, back, q0, qn)
            return remote(half, half, along(order[k], (1, 3)[j]), ssem.at[m], rsem.at[m])

        def send(k):
            for i in range(len(parts)):
                for j in range(2):
                    direct(k, i, j).start()

        def forward(k):
            for i, (r0, n, h, order) in enumerate(parts):
                m = number(k, i)
                for j, back in ((0, 3), (1, 1)):
                    got = part_view(order, k, back, r0, n)
                    remote(got, got, along(order[k], 1), ssem.at[m + j], rsem.at[m + j]).wait_recv()
                    passed(k, i, j, back).start()
                    if sib:
                        sib(got, 3 + k * 9 + i * 2 + j).start()

        def finish(k):
            for i, (r0, n, h, order) in enumerate(parts):
                for j in range(2):
                    passed(k, i, j, 2).wait_recv()
                if sib:
                    sib(part_view(order, k, 2, r0, n), 3 + k * 9 + 6 + i).start()

        def sent():
            for k in range(phases):
                for i in range(len(parts)):
                    for j in range(2):
                        direct(k, i, j).wait_send()
                        passed(k, i, j, 2).wait_send()

        def pair_views(c):
            views = [part_view(order, 0, 0, r0, n, c) for (r0, n, h, order) in parts]
            for k in range(phases):
                for r0, n, h, order in parts:
                    views.append(part_view(order, k, 3, r0, n, c))
                    views.append(part_view(order, k, 1, r0, n, c))
                for r0, n, h, order in parts:
                    views.append(part_view(order, k, 2, r0, n, c))
            return views

        return send, forward, finish, sent, pair_views

    row_send_step, row_forward, row_finish, row_sent, _ = gather(
        PARTS2,
        lambda at, r0, n, c: r0_ref.at[at["y"], at["x"], pl.ds(r0, n), :],
        lambda r0, n: r0_ref.at[y, x, pl.ds(r0, n), :],
        row_send, row_recv,
    )

    def row_begin():
        @pl.when(jnp.logical_not(is_root))
        def _():
            remote(r0_ref.at[y, x], r0_ref.at[y, x], (0, source_col), rs_send.at[0], sc_recv.at[2]).wait_recv()

        row_send_step(0)

    def chol_one(p, carry):
        factor_panel(p, s_ref, x11_ref, u_ref)
        here = pl.ds(pl.multiple_of(p * 128, 128), 128)
        x_ref[here, :] = x11_ref[here, :]
        for k in range(4):

            @pl.when(p == k)
            def _(k=k):
                panel_trees[k][0]()
                panel_to_sibling(k).start()

        return carry

    @pl.when(is_root)
    def _():
        lax.fori_loop(0, 4, chol_one, 0)

    @pl.when((core == 0) & jnp.logical_not(is_root))
    def _():
        for p, s in (
            (0, 0), (0, 1), (1, 0), (0, 2), (1, 1), (2, 0), (1, 2), (2, 1), (3, 0), (2, 2), (3, 1), (3, 2)
        ):
            panel_trees[p][1](s)
            if s == 2:
                panel_to_sibling(p).start()

    @pl.when(core == 1)
    def _():
        for i in range(2):

            @pl.when(col == i)
            def _(i=i):
                @pl.when(row == 1)
                def _():
                    local(quarter(0, 0), tile_block(i, 0))

                @pl.when(row != 1)
                def _():
                    hand_over(i, z).wait_recv()

                tile_trees[i][0]()

        for s in range(2):
            for i in range(2):
                tile_trees[i][1](s)
        for i in range(2):
            for k in range(3):
                tile_along(i, k).start()
        for i in range(2):
            for k in range(3):
                tile_from(i, k).wait_recv()
            tile_to_sibling(i).start()
        for p in range(4):
            panel_to_sibling(p).wait_recv()

    @pl.when(core == 0)
    def _():
        for i in range(2):
            tile_to_sibling(i).wait_recv()

    for which in range(2):

        @pl.when(row != which)
        def _(which=which):
            ref = c0_ref.at[core, z] if which == 0 else own_ref
            remote(ref, ref, (which, col), sc_send.at[0], sc_recv.at[which]).wait_recv()

    local(c0_ref.at[core, z], blk_ref)
    lower10 = dot_nt(a10_ref[...], x_ref[...])
    own_ref[...] = own_ref[...] - dot(lower10, dot(x_ref[...], blk_ref[...]))
    s11 = a11_ref[...] - dot_nt(lower10, lower10)

    def to_sib(ref, i):
        return remote(ref, ref, sibling, sib_send.at[i], sib_recv.at[i])

    def own_part(r0, n):
        return own_ref.at[pl.ds(r0, n), :]

    send, forward, finish, sent, pair_views = gather(
        PARTS3,
        lambda at, r0, n, c: g_ref.at[at["z"], at["y"], at["x"], c, pl.ds(r0, n), :],
        own_part, ag_send, ag_recv, to_sib,
    )
    send(0)
    local(own_ref, g_ref.at[z, y, x, core])
    for i, (r0, n, h, order) in enumerate(PARTS3):
        to_sib(g_ref.at[z, y, x, core, pl.ds(r0, n), :], i).start()
    s_ref[...] = s11
    unit(x11_ref)
    row_begin()

    def line_copy(k):
        ref = c0_ref.at[core, z]
        return remote(ref, ref, along("z", k + 1), c_send.at[k], c_recv.at[k])

    def line_from(k):
        ref = c0_ref.at[core, (z + 3 - k) % 4]
        return remote(ref, ref, along("z", 3 - k), c_send.at[k], c_recv.at[k])

    def line_to_sibling(m):
        return remote(c0_ref.at[m], c0_ref.at[m], sibling, c_send.at[3], c_recv.at[3])

    forward(0)
    finish(0)
    send(1)
    for k in range(3):
        line_copy(k).start()
    row_forward(0)
    row_finish(0)
    row_send_step(1)

    def chol_two(p, carry):
        factor_panel(p, s_ref, x11_ref, u11_ref)

        @pl.when(p == 1)
        def _():
            forward(1)

        @pl.when(p == 2)
        def _():
            finish(1)
            send(2)
            row_forward(1)

        return carry

    lax.fori_loop(0, 4, chol_two, 0)
    row_finish(1)
    for k in range(3):
        line_from(k).wait_recv()
    line_to_sibling(core).start()
    forward(2)
    finish(2)

    x00_out[...] = x_ref[...]
    x11_out[...] = x11_ref[...]
    u00_out[...] = u_ref[...]
    u11_out[...] = u11_ref[...]

    sent()
    row_sent()
    for i, v in enumerate(pair_views(core)):
        to_sib(v, i).wait_send()
    for i, v in enumerate(pair_views(1 - core)):
        to_sib(v, i).wait_recv()

    @pl.when(core == 0)
    def _():
        for p in range(4):
            panel_trees[p][2]()
            panel_to_sibling(p).wait_send()

    @pl.when(core == 1)
    def _():
        for i in range(2):
            tile_trees[i][2]()
            for k in range(3):
                tile_along(i, k).wait_send()
            tile_to_sibling(i).wait_send()

            @pl.when((row == 1) & (col == i))
            def _(i=i):
                for q in range(1, 4):
                    hand_over(i, q).wait_send()

    for k in range(3):
        line_copy(k).wait_send()
    line_to_sibling(core).wait_send()
    line_to_sibling(1 - core).wait_recv()

    @pl.when(row < 2)
    def _():
        for m in range(2):
            for q in range(4):
                pl.when(jnp.logical_not(spread_self(m, q)))(spread_copy(m, q, 1).wait_send)

    @pl.when(row == 0)
    def _():
        for m in range(2):
            for q in range(4):
                pl.when(jnp.logical_not(row_self(m, q)))(row_copy(m, q).wait_send)


def split(v):
    high = v.astype(BF16)
    return high, (v - high.astype(F32)).astype(BF16)


def dot16(a, b):
    return lax.dot_general(a, b, (((1,), (0,)), ((), ())), preferred_element_type=F32)


def left_parts(v):
    high, low = split(v)
    return jnp.concatenate([high, high, low], 1)


def right_parts(v):
    high, low = split(v)
    return jnp.concatenate([high, low, high], 0)


def finish_kernel(
    plan_ref, cov_ref, g_ref, r0_ref, c0_ref, x00_ref, x11_ref, u00_ref, u11_ref,
    f_ref, o_ref,
    x_buf, xt_ref, xb_ref, row_buf, col_buf, tile_buf, left_ref, right_ref, half_buf, out_buf, zero_buf,
    x_sem, row_sem, col_sem, tile_sem, f_sem, half_sem, o_sem,
):
    row = lax.axis_index("row")
    col = lax.axis_index("col")

    def panel_tile(i):
        return g_ref.at[:, (i % 16) // 4, i % 4, i // 16]

    def row_copy(l, k):
        src = r0_ref.at[l] if k == 0 else panel_tile(l * 8 + row)
        return pltpu.make_async_copy(src, row_buf.at[k, l], row_sem.at[k, l])

    def col_copy(m, k):
        src = c0_ref.at[m] if k == 0 else panel_tile(m * 16 + col)
        return pltpu.make_async_copy(src, col_buf.at[k, m], col_sem.at[k, m])

    def tile_copy(n):
        return pltpu.make_async_copy(cov_ref.at[n // 2, n % 2], tile_buf.at[n], tile_sem.at[n])

    def f_copy(n):
        return pltpu.make_async_copy(tile_buf.at[n], f_ref.at[n // 2, n % 2], f_sem.at[n])

    def place(n):
        return (n // 2) * 8 + row, (n % 2) * 16 + col

    def updated(n):
        i, j = place(n)
        return (j > 1) & (i >= j)

    def entry(s):
        t = plan_ref[s]
        u = jnp.maximum(t, 0)
        return t >= 0, u // 4, (u // 2) % 2, u % 2

    def half_copy(s):
        _, _, m, h = entry(s)
        src = g_ref.at[pl.ds(2 * h, 2), s // 4, s % 4, m]
        return pltpu.make_async_copy(src, half_buf.at[s % 2], half_sem.at[s % 2])

    def x_copy(k):
        return pltpu.make_async_copy((x00_ref, x11_ref)[k], x_buf.at[k], x_sem.at[k])

    for k in range(2):
        x_copy(k).start()
    for m in range(2):
        for k in range(2):
            col_copy(m, k).start()
    for l in range(4):
        for k in range(2):
            row_copy(l, k).start()
    for n in range(8):
        pl.when(updated(n))(tile_copy(n).start)
    pl.when(entry(0)[0])(lambda: half_copy(0).start())

    for k in range(2):
        x_copy(k).wait()
        xt_ref[k] = left_parts(x_buf[k, :HALF, :HALF])
        xb_ref[k] = left_parts(x_buf[k, HALF:, :])
    zero_buf[...] = jnp.zeros((NB, HALF), F32)

    def solved(k, blocks):
        tile = jnp.concatenate(blocks, 1)
        top = dot16(xt_ref[k], right_parts(tile[:HALF]))
        return jnp.concatenate([top, dot16(xb_ref[k], right_parts(tile))], 0)

    def make_col(m, carry):
        for k in range(2):
            col_copy(m, k).wait()
            right_ref[m, 3 * k * NB : 3 * (k + 1) * NB, :] = right_parts(
                solved(k, [col_buf[k, m, q] for q in range(4)])
            )
        return carry

    lax.fori_loop(0, 2, make_col, 0)

    def make_row(l, carry):
        for k in range(2):
            row_copy(l, k).wait()
            p = solved(k, [row_buf[k, l, q] for q in range(4)]).T
            left_ref[l, :, 3 * k * NB : 3 * (k + 1) * NB] = left_parts(p)
            i = l * 8 + row

            @pl.when(col == k)
            def _():
                tile_buf[2 * l] = p

                @pl.when(i == k)
                def _():
                    factor = pltpu.make_async_copy((u00_ref, u11_ref)[k], x_buf.at[k], x_sem.at[k])
                    factor.start()
                    factor.wait()
                    tile_buf[2 * l] = x_buf[k].T

                @pl.when(i < k)
                def _():
                    tile_buf[2 * l] = jnp.zeros((NB, NB), F32)

        return carry

    lax.fori_loop(0, 4, make_row, 0)

    def trailing(n, carry):
        i, j = place(n)
        l, m = n // 2, n % 2

        @pl.when(updated(n))
        def _():
            tile_copy(n).wait()
            tile_buf[n] = tile_buf[n] - dot16(left_ref[l], right_ref[m])

        @pl.when((j > 1) & (i < j))
        def _():
            tile_buf[n] = jnp.zeros((NB, NB), F32)

        f_copy(n).start()
        return carry

    lax.fori_loop(0, 8, trailing, 0)

    def out_copy(s):
        return pltpu.make_async_copy(out_buf.at[s % 2], o_ref.at[s], o_sem.at[s % 2])

    def moved(s, carry):
        live, l, m, h = entry(s)

        @pl.when(s >= 2)
        def _():
            out_copy(s).wait()

        @pl.when((s < 15) & entry(jnp.minimum(s + 1, 15))[0])
        def _():
            half_copy(jnp.minimum(s + 1, 15)).start()

        @pl.when(live)
        def _():
            half_copy(s).wait()
            right = right_parts(solved(1, [half_buf[s % 2, q] for q in range(2)]))
            out_buf[s % 2] = dot16(left_ref[l, :, 3 * NB :], right)
            out_copy(s).start()

        @pl.when(jnp.logical_not(live))
        def _():
            pltpu.make_async_copy(zero_buf, o_ref.at[s], o_sem.at[s % 2]).start()

        return carry

    lax.fori_loop(0, 16, moved, 0)
    for s in (14, 15):
        out_copy(s).wait()
    for n in range(8):
        f_copy(n).wait()


def per_device(covariance, migration):
    cov = covariance.reshape(4, 2, NB, NB)
    row = lax.axis_index("row")
    col = lax.axis_index("col")
    plan = lax.dynamic_slice(migration, (row, 0, col), (1, 16, 1)).reshape(16)
    dma = pltpu.SemaphoreType.DMA
    square = jax.ShapeDtypeStruct((NB, NB), F32)
    g, r0, c0, x00, x11, u00, u11 = pl.pallas_call(
        exchange_kernel,
        out_shape=[
            jax.ShapeDtypeStruct((4, 4, 4, 2, NB, QB), F32),
            jax.ShapeDtypeStruct((4, 4, NB, QB), F32),
            jax.ShapeDtypeStruct((2, 4, NB, QB), F32),
            square, square, square, square,
        ],
        in_specs=[ANY],
        out_specs=[ANY] * 3 + [VMEM] * 4,
        scratch_shapes=[pltpu.VMEM((NB, NB), F32)] * 7
        + [pltpu.VMEM((NB, QB), F32)] * 2
        + [
            dma, dma((4,)), dma((2,)), dma((2, 3)), dma((2, 3)), dma((8,)), dma((3,)), dma((8,)),
            dma((4, 3, 9)), dma((4, 3)), dma((2, 2, 6)), dma((2, 2)),
            dma((16,)), dma((16,)), dma((36,)), dma((36,)), dma((30,)), dma((30,)),
            dma((4,)), dma((4,)), dma((6,)), dma((6,)),
        ],
        compiler_params=pltpu.CompilerParams(
            collective_id=0, has_side_effects=True, vmem_limit_bytes=48 * 2**20
        ),
        name="exchange",
    )(cov)
    factor, offloaded = pl.pallas_call(
        finish_kernel,
        out_shape=[
            jax.ShapeDtypeStruct((4, 2, NB, NB), F32),
            jax.ShapeDtypeStruct((16, NB, HALF), F32),
        ],
        in_specs=[SMEM] + [ANY] * 8,
        out_specs=[ANY, ANY],
        scratch_shapes=[
            pltpu.VMEM((2, NB, NB), F32), pltpu.VMEM((2, HALF, 3 * HALF), BF16), pltpu.VMEM((2, HALF, 3 * NB), BF16),
            pltpu.VMEM((2, 4, 4, NB, QB), F32), pltpu.VMEM((2, 2, 4, NB, QB), F32),
            pltpu.VMEM((8, NB, NB), F32),
            pltpu.VMEM((4, NB, 6 * NB), BF16), pltpu.VMEM((2, 6 * NB, NB), BF16),
            pltpu.VMEM((2, 2, NB, QB), F32), pltpu.VMEM((2, NB, HALF), F32), pltpu.VMEM((NB, HALF), F32),
            dma((2,)), dma((2, 4)), dma((2, 2)), dma((8,)), dma((8,)), dma((2,)), dma((2,)),
        ],
        compiler_params=pltpu.CompilerParams(vmem_limit_bytes=60 * 2**20),
        name="finish",
    )(plan, cov, g, r0, c0, x00, x11, u00, u11)
    return factor[:, None, :, None], offloaded[None, None]


def solution(mesh):
    return jax.shard_map(
        per_device,
        mesh=mesh,
        in_specs=(P(None, "row", None, "col", None, None), P()),
        out_specs=(P(None, "row", None, "col", None, None), P("row", "col", None, None, None)),
        check_vma=False,
    )
```
